512 devices in a mesh: row: 16 (over x, y), col: 32 (over z, core).
Axes of the slice: x: 4, y: 4, z: 16, core: 2. Of those that a mesh axis runs over, the one named last changes fastest.
Arguments:
- inputs: bfloat16 [2048, 25600], P('row', 'col'), may hold values from -6 to 6
- out_grads: bfloat16 [2048, 5120], P('col', 'row'), may hold values from -0.125 to 0.125
- weights: bfloat16 [5120, 25600], P('row', 'col'), may hold values from -3 to 3
- momentum: float32 [5120, 25600], P('row', 'col'), may hold values from -13 to 13
- right_factor: float32 [25600, 256], P('col'), may hold values from -6 to 6
Outputs:
- weights_new: float32 [5120, 25600], P('row', 'col')
- momentum_new: float32 [5120, 25600], P('row', 'col')
- factor_new: float32 [25600, 256], P('col')
The draws below stay inside these ranges and needn't reach their ends.
All inputs are finite; a program needn't handle non-finite values.
Results may differ from the reference program's by a relative error of at most 0.0003.
Values may be sent and summed in bfloat16 or wider, within the bound.
A program may use at most 64 MiB of HBM per device.

```python
import math
import jax
import jax.numpy as jnp
from jax import lax

M = 5120
N = 25600
RANK = 256
TOKENS = 2048


def draw_momentum(key, part):
    keys = jax.random.split(jax.random.fold_in(key, 7), 3)
    row_scale = jnp.exp(jax.random.uniform(keys[0], (M, 1), jnp.float32, -0.58, 0.58))
    col_scale = jnp.exp(jax.random.uniform(keys[1], (1, N), jnp.float32, -0.58, 0.58))
    base = jnp.clip(jax.random.normal(keys[2], (M, N), jnp.float32), -4.0, 4.0)
    return base * row_scale * col_scale


def block_scale(own_key, shape, cuts, low, largest):
    level, own = 1.0, jax.random.fold_in(own_key, 6)
    for axis_at, blocks in cuts:
        draws = jnp.exp(jax.random.uniform(jax.random.fold_in(own, axis_at), (blocks,), jnp.float32, low / len(cuts), largest / len(cuts)))
        level = level * jnp.repeat(draws, shape[axis_at] // blocks).reshape([-1 if axis == axis_at else 1 for axis in range(len(shape))])
    return level


def scatter_about(own_key, extent, deviation, most, cuts=(), dtype=jnp.bfloat16):
    level = block_scale(own_key, extent, cuts, -0.22, 0.18) if cuts else 1.0
    result = jax.random.normal(own_key, extent, jnp.float32) * deviation * level
    return jnp.minimum(jnp.maximum(result, -most), most).astype(dtype)


def setup_inputs(seed: int = 0) -> dict:
    arg_keys = jax.random.split(jax.random.key(seed), 6)
    return {
        "inputs": scatter_about(arg_keys[0], (TOKENS, N), 1.0, 6.0, ((0, 16), (1, 32))),
        "out_grads": scatter_about(arg_keys[1], (TOKENS, M), TOKENS ** -0.5, 0.125, ((0, 32), (1, 16))),
        "weights": scatter_about(arg_keys[2], (M, N), 0.5, 3.0, ((0, 16), (1, 32))),
        "momentum": draw_momentum(jax.random.fold_in(arg_keys[5], 71), 0),
        "right_factor": scatter_about(arg_keys[4], (N, RANK), 1.0, 6.0, ((0, 32),), jnp.float32),
    }


mix_rate = 0.95
step_rate = 0.3
weight_decay = 0.1
tiny_eps = 1e-06
highest = lax.Precision.HIGHEST

def reference(inputs, out_grads, weights, momentum, right_factor):
    gradient = jnp.dot(out_grads.T.astype(jnp.float32), inputs.astype(jnp.float32), preferred_element_type=jnp.float32)
    moment = momentum + gradient
    sketch = jnp.dot(moment, right_factor, precision=highest)
    gram = jnp.dot(sketch.T, sketch, precision=highest)
    factor_low = jnp.linalg.cholesky(gram)
    basis = jax.scipy.linalg.solve_triangular(factor_low, sketch.T, lower=True).T
    right_side = jnp.dot(moment.T, basis, precision=highest)
    column_scale = lax.rsqrt(lax.optimization_barrier(jnp.sum(right_side * right_side, axis=0)) / N + tiny_eps)
    factor_new = right_side * column_scale
    momentum_new = moment - (1.0 - mix_rate) * jnp.dot(basis, right_side.T, precision=highest)
    update = jnp.dot(basis, factor_new.T, precision=highest)
    weights_new = weights.astype(jnp.float32) * (1.0 - step_rate * weight_decay) - step_rate * math.sqrt(M / RANK) * update
    return (weights_new, momentum_new, factor_new)
```

```python
import functools
import math

import jax
import jax.numpy as jnp
from jax import lax
from jax.experimental import pallas as pl
from jax.experimental.pallas import tpu as pltpu
from jax.sharding import PartitionSpec as P

M = 5120
N = 25600
RANK = 256
TOKENS = 2048

mix_rate = 0.95
step_rate = 0.3
weight_decay = 0.1
tiny_eps = 1e-06
highest = lax.Precision.HIGHEST
MESH = pl.DeviceIdType.MESH
f32 = jnp.float32
bf16 = jnp.bfloat16
VMEM_LIMIT = 56 * 2**20
XY = [(a, b) for a in range(4) for b in range(4) if (a, b) != (0, 0)]


def place():
    r = lax.axis_index("row")
    c = lax.axis_index("col")
    return r // 4, r % 4, c // 2, c % 2


def at(x, y, z, k):
    return (x * 4 + y, z * 2 + k)


def moved(dx=0, dy=0, dz=0, dk=0):
    x, y, z, k = place()
    return at((x + dx) % 4, (y + dy) % 4, (z + dz) % 16, (k + dk) % 2)


def greet(offsets):
    barrier = pltpu.get_barrier_semaphore()
    for o in offsets:
        pl.semaphore_signal(barrier, inc=1, device_id=moved(*o), device_id_type=MESH)
    return lambda: pl.semaphore_wait(barrier, len(offsets))


def send(src, dst, send_sem, recv_sem, to):
    copy = pltpu.make_async_remote_copy(
        src_ref=src, dst_ref=dst, send_sem=send_sem, recv_sem=recv_sem, device_id=to, device_id_type=MESH
    )
    copy.start()
    return copy


def landed(dst, recv_sem, send_sem):
    pltpu.make_async_remote_copy(
        src_ref=dst, dst_ref=dst, send_sem=send_sem, recv_sem=recv_sem, device_id=moved(0, 0, 0, 1), device_id_type=MESH
    ).wait_recv()


def dot(a, b, ca, cb):
    return lax.dot_general(a, b, (((ca,), (cb,)), ((), ())), precision=highest, preferred_element_type=f32)


def sketch_kernel(
    x_ref, g_ref, m_ref, r_ref,
    moment_ref, s_out, gram_out,
    xall, gall, rt, acc, sp, pair, cs, rs, sall, gp, grs, gall2,
    own_sem, xs_sem, xa_sem, xb_sem, gs_sem, gr_sem, gd_sem, gk_sem,
    p_sem, zs_sem, zr_sem, as_sem, ar_sem, ak_sem, hs_sem, hr_sem, ts_sem, tr_sem,
):
    x, y, z, k = place()
    row = x * 4 + y
    ready = greet(
        [(a, b, 0, j) for a in range(4) for b in range(4) for j in range(2) if (a, b, j) != (0, 0, 0)]
        + [(0, 0, d, 0) for d in range(1, 16)]
    )
    own_x = pltpu.make_async_copy(x_ref, xall.at[row], own_sem.at[0])
    own_g = pltpu.make_async_copy(g_ref, gall.at[k, z], own_sem.at[1])
    own_x.start()
    own_g.start()
    rt[...] = r_ref[...].T
    own_x.wait()
    own_g.wait()
    ready()

    sent = []
    number = 0

    def half(which, owner):
        return xall.at[owner, pl.ds(64 * which, 64)]

    def pass_on(which, owner, along_x):
        nonlocal number
        sem = xb_sem if which else xa_sem
        for d in range(1, 4):
            to = moved(d, 0) if along_x else moved(0, d)
            sent.append(send(half(which, owner), half(which, owner), xs_sem.at[number], sem.at[owner], to))
            number += 1

    gnum = 0

    def pass_g(owner, ds):
        nonlocal gnum
        for d in ds:
            sent.append(
                send(gall.at[k, owner], gall.at[k, owner], gs_sem.at[gnum], gr_sem.at[owner], moved(0, 0, d))
            )
            gnum += 1

    pass_g(z, (4, 8, 12))
    pass_on(0, row, True)
    pass_on(1, row, False)
    pass_g(z, (1, 2, 15))
    pass_on(0, row, False)
    pass_on(1, row, True)
    for d in (1, 3, 2):
        ox = ((x + 4 - d) % 4) * 4 + y
        oy = x * 4 + (y + 4 - d) % 4
        landed(half(0, ox), xa_sem.at[ox], xs_sem.at[0])
        pass_on(0, ox, False)
        landed(half(1, oy), xb_sem.at[oy], xs_sem.at[0])
        pass_on(1, oy, True)
    for d in (4, 12, 8):
        oz = (z + 16 - d) % 16
        landed(gall.at[k, oz], gr_sem.at[oz], gs_sem.at[0])
        pass_g(oz, (1, 2, 15))
    for a in (0, 4, 8, 12):
        for d in (1, 2, 15):
            oz = (z + 16 - d + 16 - a) % 16
            landed(gall.at[k, oz], gr_sem.at[oz], gs_sem.at[0])
    sent.append(send(gall.at[k], gall.at[k], gd_sem.at[0], gk_sem.at[0], moved(0, 0, 0, 1)))
    landed(gall.at[1 - k], gk_sem.at[0], gd_sem.at[0])

    acc[...] = m_ref[...]
    waited = [(0, 0)]
    for dx in (0, 1, 3, 2):
        gx = (x + 4 - dx) % 4
        for dy in range(4):
            owner = gx * 4 + (y + 4 - dy) % 4
            if dy != 0:
                if dx != 0:
                    landed(half(0, owner), xa_sem.at[owner], xs_sem.at[0])
                    landed(half(1, owner), xb_sem.at[owner], xs_sem.at[0])
                else:
                    landed(half(0, owner), xa_sem.at[owner], xs_sem.at[0])
            elif dx != 0:
                landed(half(1, owner), xb_sem.at[owner], xs_sem.at[0])
        xs = xall[pl.ds(gx * 4, 4)].reshape(4, 2, 64, 800)
        total = None
        for j in range(2):
            gs = gall[j, pl.ds(gx * 4, 4)].reshape(256, 320)
            part = lax.dot_general(
                gs, xs[:, j].reshape(256, 800), (((0,), (0,)), ((), ())), preferred_element_type=f32
            )
            total = part if total is None else total + part
        acc[...] += total
    moment_ref[...] = acc[...]
    sp[...] = dot(rt[...], acc[...], 1, 1).reshape(2, 16, 8, 320)

    c = send(sp.at[1 - k], pair, p_sem.at[0], p_sem.at[1], moved(0, 0, 0, 1))
    c.wait()
    cs[...] = sp[k] + pair[...]
    copies = [
        send(cs.at[(z + d) % 16], rs.at[d], zs_sem.at[d], zr_sem.at[d], moved(0, 0, d)) for d in range(1, 16)
    ]
    total = cs[z]
    for d in range(1, 16):
        copies[d - 1].wait_recv()
        total = total + rs[d]
    sall[k, z] = total
    sent += copies
    for d in range(1, 16):
        sent.append(send(sall.at[k, z], sall.at[k, z], as_sem.at[d], ar_sem.at[z], moved(0, 0, d)))
    for d in range(1, 16):
        oz = (z + 16 - d) % 16
        landed(sall.at[k, oz], ar_sem.at[oz], as_sem.at[0])
    sent.append(send(sall.at[k], sall.at[k], ak_sem.at[0], ak_sem.at[1], moved(0, 0, 0, 1)))
    landed(sall.at[1 - k], ak_sem.at[1], ak_sem.at[0])

    s_all = sall[...].reshape(256, 320)
    s_out[...] = s_all
    gp[...] = dot(sall[k].reshape(128, 320), s_all, 1, 1).reshape(16, 8, 256)
    copies = []
    for i, (a, b) in enumerate(XY):
        to_row = ((x + a) % 4) * 4 + (y + b) % 4
        copies.append(send(gp.at[to_row], grs.at[i], hs_sem.at[i], hr_sem.at[i], moved(a, b)))
    total = gp[row]
    for i in range(15):
        copies[i].wait_recv()
        total = total + grs[i]
    gall2[k, row] = total
    sent += copies
    n = 0
    for j in range(2):
        for a, b in [(0, 0)] + XY:
            if (a, b, j) != (0, 0, 0):
                sent.append(
                    send(gall2.at[k, row], gall2.at[k, row], ts_sem.at[n], tr_sem.at[k, row], moved(a, b, 0, j))
                )
                n += 1
    for j in range(2):
        for a, b in [(0, 0)] + XY:
            if (a, b, j) != (0, 0, 0):
                owner = ((x + 4 - a) % 4) * 4 + (y + 4 - b) % 4
                kk = (k + j) % 2
                landed(gall2.at[kk, owner], tr_sem.at[kk, owner], ts_sem.at[0])
    gram_out[...] = gall2[...].reshape(256, 256)
    for c in sent:
        c.wait_send()


def wide(column):
    return jnp.broadcast_to(column, (8, 128))


def factor_64(tile, parity):
    sub = lax.broadcasted_iota(jnp.int32, (8, 128), 0)
    rows = [tile[8 * t : 8 * t + 8] for t in range(8)]
    for p in range(8):
        first = 64 * parity + 8 * p
        col = {t: [wide(rows[t][:, first + j : first + j + 1]) for j in range(8)] for t in range(p, 8)}
        pivots = jnp.ones((8, 128), f32)
        for j in range(8):
            b = {i: wide(col[p][j][i : i + 1]) for i in range(j, 8)}
            inverse = 1.0 / b[j]
            pivots = jnp.where(sub == j, b[j], pivots)
            line = wide(rows[p][j : j + 1])
            for t in range(p, 8):
                factor = col[t][j] * inverse
                if t == p:
                    factor = jnp.where(sub > j, factor, 0.0)
                for i in range(j + 1, 8):
                    col[t][i] = col[t][i] - factor * b[i]
                rows[t] = rows[t] - factor * line
        rows[p] = rows[p] * lax.rsqrt(pivots)
    return jnp.concatenate(rows, axis=0)


def basis_kernel(gram_ref, s_ref, moment_ref, bt_ref, right_ref, ah):
    ah[:, 0:256] = gram_ref[...]
    ah[:, 256:576] = s_ref[...]
    lane = lax.broadcasted_iota(jnp.int32, (64, 128), 1)
    line = lax.broadcasted_iota(jnp.int32, (64, 128), 0)
    for b in range(4):
        parity, low = b % 2, 64 * b
        own = (lane // 64) == parity
        unit = jnp.where(lane == line + 64 * (1 - parity), 1.0, 0.0)
        tile = jnp.where(own, ah[low : low + 64, 128 * (b // 2) : 128 * (b // 2) + 128], unit)
        inverse = jnp.where(own, 0.0, factor_64(tile, parity))
        first = 128 * ((b + 1) // 2)
        block = ah[low : low + 64, first:576]
        upper = dot(inverse, jnp.concatenate([block, block], axis=0), 1, 0)
        bt_ref[low : low + 64, :] = upper[:, 256 - first :]
        if b < 3:
            change = dot(upper[:, : 256 - first], upper, 0, 0)
            ah[low + 64 : 256, first:576] = ah[low + 64 : 256, first:576] - change[low + 64 - first :, :]
    right_ref[...] = dot(bt_ref[...], moment_ref[...], 1, 0).reshape(16, 16, 800)


def right_kernel(
    part_ref, right_out, squares_out,
    rs, rall, sq, sqs, sqall,
    s_sem, r_sem, as_sem, ar_sem, qs_sem, qr_sem, ts_sem, tr_sem,
):
    x, y, z, k = place()
    row = x * 4 + y
    cols = [(0, 0, d, j) for d in range(16) for j in range(2) if (d, j) != (0, 0)]
    ready = greet([(a, b, 0, 0) for a, b in XY] + cols)
    ready()
    sent = []
    copies = []
    for i, (a, b) in enumerate(XY):
        to_row = ((x + a) % 4) * 4 + (y + b) % 4
        copies.append(send(part_ref.at[to_row], rs.at[i], s_sem.at[i], r_sem.at[i], moved(a, b)))
    total = part_ref[row]
    for i in range(15):
        copies[i].wait_recv()
        total = total + rs[i]
    sent += copies
    rall[row] = total
    for i, (a, b) in enumerate(XY):
        sent.append(send(rall.at[row], rall.at[row], as_sem.at[i], ar_sem.at[row], moved(a, b)))
    sq[...] = jnp.broadcast_to(jnp.sum(total * total, axis=1, keepdims=True), (16, 128))
    copies = [send(sq, sqs.at[i], qs_sem.at[i], qr_sem.at[i], moved(*o)) for i, o in enumerate(cols)]
    total = sq[...]
    for i in range(31):
        copies[i].wait_recv()
        total = total + sqs[i]
    sent += copies
    sqall[row] = total
    for i, (a, b) in enumerate(XY):
        sent.append(send(sqall.at[row], sqall.at[row], ts_sem.at[i], tr_sem.at[row], moved(a, b)))
    for a, b in XY:
        owner = ((x + 4 - a) % 4) * 4 + (y + 4 - b) % 4
        landed(rall.at[owner], ar_sem.at[owner], as_sem.at[0])
    right_out[...] = rall[...].reshape(256, 800)
    for a, b in XY:
        owner = ((x + 4 - a) % 4) * 4 + (y + 4 - b) % 4
        landed(sqall.at[owner], tr_sem.at[owner], ts_sem.at[0])
    squares_out[...] = sqall[...].reshape(256, 128)
    for c in sent:
        c.wait_send()


def update_kernel(w_ref, moment_ref, bt_ref, right_ref, squares_ref, w_out, m_out, f_out):
    scale = lax.rsqrt(squares_ref[...][:, :1] / N + tiny_eps)
    basis = bt_ref[...].T
    right = right_ref[...]
    m_out[...] = moment_ref[...] - (1.0 - mix_rate) * dot(basis, right, 1, 0)
    factor = right * scale
    f_out[...] = factor.T
    w_out[...] = w_ref[...].astype(f32) * (1.0 - step_rate * weight_decay) - step_rate * math.sqrt(
        M / RANK
    ) * dot(basis, factor, 1, 0)


def vmem(count):
    return [pl.BlockSpec(memory_space=pltpu.VMEM)] * count


def shape(*dims):
    return jax.ShapeDtypeStruct(dims, f32)


def on_device(inputs, out_grads, weights, momentum, right_factor):
    dma = pltpu.SemaphoreType.DMA
    moment, sketch, gram = pl.pallas_call(
        sketch_kernel,
        name="sketch",
        out_shape=(shape(320, 800), shape(256, 320), shape(256, 256)),
        in_specs=vmem(4),
        out_specs=tuple(vmem(3)),
        scratch_shapes=[
            pltpu.VMEM((16, 128, 800), bf16),
            pltpu.VMEM((2, 16, 64, 320), bf16),
            pltpu.VMEM((256, 800), f32),
            pltpu.VMEM((320, 800), f32),
            pltpu.VMEM((2, 16, 8, 320), f32),
            pltpu.VMEM((16, 8, 320), f32),
            pltpu.VMEM((16, 8, 320), f32),
            pltpu.VMEM((16, 8, 320), f32),
            pltpu.VMEM((2, 16, 8, 320), f32),
            pltpu.VMEM((16, 8, 256), f32),
            pltpu.VMEM((15, 8, 256), f32),
            pltpu.VMEM((2, 16, 8, 256), f32),
            dma((2,)), dma((30,)), dma((16,)), dma((16,)), dma((15,)), dma((16,)), dma((1,)), dma((1,)),
            dma((2,)), dma((16,)), dma((16,)), dma((16,)), dma((16,)), dma((2,)), dma((15,)), dma((15,)),
            dma((31,)), dma((2, 16)),
        ],
        compiler_params=pltpu.CompilerParams(collective_id=0, has_side_effects=True, vmem_limit_bytes=VMEM_LIMIT),
    )(inputs, out_grads, momentum, right_factor)
    basis_t, part = pl.pallas_call(
        basis_kernel,
        name="basis",
        out_shape=(shape(256, 320), shape(16, 16, 800)),
        in_specs=vmem(3),
        out_specs=tuple(vmem(2)),
        scratch_shapes=[pltpu.VMEM((256, 576), f32)],
        compiler_params=pltpu.CompilerParams(vmem_limit_bytes=VMEM_LIMIT),
    )(gram, sketch, moment)
    right, squares = pl.pallas_call(
        right_kernel,
        name="right_side",
        out_shape=(shape(256, 800), shape(256, 128)),
        in_specs=vmem(1),
        out_specs=tuple(vmem(2)),
        scratch_shapes=[
            pltpu.VMEM((15, 16, 800), f32),
            pltpu.VMEM((16, 16, 800), f32),
            pltpu.VMEM((16, 128), f32),
            pltpu.VMEM((31, 16, 128), f32),
            pltpu.VMEM((16, 16, 128), f32),
            dma((15,)), dma((15,)), dma((15,)), dma((16,)), dma((31,)), dma((31,)), dma((15,)), dma((16,)),
        ],
        compiler_params=pltpu.CompilerParams(collective_id=1, has_side_effects=True, vmem_limit_bytes=VMEM_LIMIT),
    )(part)
    return tuple(
        pl.pallas_call(
            update_kernel,
            name="updates",
            out_shape=(shape(320, 800), shape(320, 800), shape(800, 256)),
            in_specs=vmem(5),
            out_specs=tuple(vmem(3)),
            compiler_params=pltpu.CompilerParams(vmem_limit_bytes=VMEM_LIMIT),
        )(weights, moment, basis_t, right, squares)
    )


def solution(mesh):
    return jax.shard_map(
        on_device,
        mesh=mesh,
        in_specs=(P("row", "col"), P("col", "row"), P("row", "col"), P("row", "col"), P("col", None)),
        out_specs=(P("row", "col"), P("row", "col"), P("col", None)),
        check_vma=False,
    )
```

```python
import functools
import math

import jax
import jax.numpy as jnp
from jax import lax
from jax.experimental import pallas as pl
from jax.experimental.pallas import tpu as pltpu
from jax.sharding import PartitionSpec as P

M = 5120
N = 25600
RANK = 256
TOKENS = 2048

mix_rate = 0.95
step_rate = 0.3
weight_decay = 0.1
tiny_eps = 1e-06
highest = lax.Precision.HIGHEST
MESH = pl.DeviceIdType.MESH
f32 = jnp.float32
bf16 = jnp.bfloat16
VMEM_LIMIT = 56 * 2**20
XY = [(a, b) for a in range(4) for b in range(4) if (a, b) != (0, 0)]


def place():
    r = lax.axis_index("row")
    c = lax.axis_index("col")
    return r // 4, r % 4, c // 2, c % 2


def at(x, y, z, k):
    return (x * 4 + y, z * 2 + k)


def moved(dx=0, dy=0, dz=0, dk=0):
    x, y, z, k = place()
    return at((x + dx) % 4, (y + dy) % 4, (z + dz) % 16, (k + dk) % 2)


def greet(offsets):
    barrier = pltpu.get_barrier_semaphore()
    for o in offsets:
        pl.semaphore_signal(barrier, inc=1, device_id=moved(*o), device_id_type=MESH)
    return lambda: pl.semaphore_wait(barrier, len(offsets))


def send(src, dst, send_sem, recv_sem, to):
    copy = pltpu.make_async_remote_copy(
        src_ref=src, dst_ref=dst, send_sem=send_sem, recv_sem=recv_sem, device_id=to, device_id_type=MESH
    )
    copy.start()
    return copy


def landed(dst, recv_sem, send_sem):
    pltpu.make_async_remote_copy(
        src_ref=dst, dst_ref=dst, send_sem=send_sem, recv_sem=recv_sem, device_id=moved(0, 0, 0, 1), device_id_type=MESH
    ).wait_recv()


def dot(a, b, ca, cb):
    return lax.dot_general(a, b, (((ca,), (cb,)), ((), ())), precision=highest, preferred_element_type=f32)


def step_kernel(
    x_ref, g_ref, m_ref, r_ref,
    moment_ref, bt_ref, right_out, squares_out,
    xall, gall, rt, acc, sp, pair, cs, rs, sall, gp, grs, gall2, ah,
    part, brs, rall, sq, sq2, sqs, sqall,
    own_sem, xs_sem, xa_sem, xb_sem, gs_sem, gr_sem, gd_sem, gk_sem,
    p_sem, zs_sem, zr_sem, as_sem, ar_sem, ak_sem, hs_sem, hr_sem, ts_sem, tr_sem,
    bs_sem, br_sem, cs_sem, cr_sem, qp_sem, qs_sem, qr_sem, us_sem, ur_sem,
):
    x, y, z, k = place()
    row = x * 4 + y
    ready = greet(
        [(0, 0, d, 0) for d in (8, 7, 9, 6, 10, 5, 11, 4, 12, 3, 13, 2, 14, 1, 15)]
        + [(a, b, 0, 0) for a, b in XY[::-1]]
        + [(0, 0, 0, 1)]
    )
    own_x = pltpu.make_async_copy(x_ref, xall.at[row], own_sem.at[0])
    own_g = pltpu.make_async_copy(g_ref, gall.at[k, z], own_sem.at[1])
    own_x.start()
    own_g.start()
    rt[...] = r_ref[...].T
    own_x.wait()
    own_g.wait()
    ready()

    sent = []
    number = 0

    def half(which, owner):
        return xall.at[owner, pl.ds(64 * which, 64)]

    def pass_on(which, owner, along_x):
        nonlocal number
        sem = xb_sem if which else xa_sem
        for d in range(1, 4):
            to = moved(d, 0) if along_x else moved(0, d)
            sent.append(send(half(which, owner), half(which, owner), xs_sem.at[number], sem.at[owner], to))
            number += 1

    gnum = 0

    def pass_g(owner, ds):
        nonlocal gnum
        for d in ds:
            sent.append(
                send(gall.at[k, owner], gall.at[k, owner], gs_sem.at[gnum], gr_sem.at[owner], moved(0, 0, d))
            )
            gnum += 1

    pass_g(z, (4, 8, 12))
    pass_on(0, row, True)
    pass_on(1, row, False)
    pass_g(z, (1, 2, 15))
    pass_on(0, row, False)
    pass_on(1, row, True)
    for d in (1, 3, 2):
        ox = ((x + 4 - d) % 4) * 4 + y
        oy = x * 4 + (y + 4 - d) % 4
        landed(half(0, ox), xa_sem.at[ox], xs_sem.at[0])
        pass_on(0, ox, False)
        landed(half(1, oy), xb_sem.at[oy], xs_sem.at[0])
        pass_on(1, oy, True)
    for d in (4, 12, 8):
        oz = (z + 16 - d) % 16
        landed(gall.at[k, oz], gr_sem.at[oz], gs_sem.at[0])
        pass_g(oz, (1, 2, 15))
    for a in (0, 4, 8, 12):
        for d in (1, 2, 15):
            oz = (z + 16 - d + 16 - a) % 16
            landed(gall.at[k, oz], gr_sem.at[oz], gs_sem.at[0])
    sent.append(send(gall.at[k], gall.at[k], gd_sem.at[0], gk_sem.at[0], moved(0, 0, 0, 1)))
    landed(gall.at[1 - k], gk_sem.at[0], gd_sem.at[0])

    acc[...] = m_ref[...]
    waited = [(0, 0)]
    for dx in (0, 1, 3, 2):
        gx = (x + 4 - dx) % 4
        for dy in range(4):
            owner = gx * 4 + (y + 4 - dy) % 4
            if dy != 0:
                if dx != 0:
                    landed(half(0, owner), xa_sem.at[owner], xs_sem.at[0])
                    landed(half(1, owner), xb_sem.at[owner], xs_sem.at[0])
                else:
                    landed(half(0, owner), xa_sem.at[owner], xs_sem.at[0])
            elif dx != 0:
                landed(half(1, owner), xb_sem.at[owner], xs_sem.at[0])
        xs = xall[pl.ds(gx * 4, 4)].reshape(4, 2, 64, 800)
        total = None
        for j in range(2):
            gs = gall[j, pl.ds(gx * 4, 4)].reshape(256, 320)
            piece = lax.dot_general(
                gs, xs[:, j].reshape(256, 800), (((0,), (0,)), ((), ())), preferred_element_type=f32
            )
            total = piece if total is None else total + piece
        acc[...] += total
    moment_ref[...] = acc[...]
    sp[...] = dot(rt[...], acc[...], 1, 1).reshape(2, 16, 8, 320)

    c = send(sp.at[1 - k], pair, p_sem.at[0], p_sem.at[1], moved(0, 0, 0, 1))
    c.wait()
    cs[...] = sp[k] + pair[...]
    copies = [
        send(cs.at[(z + d) % 16], rs.at[d], zs_sem.at[d], zr_sem.at[d], moved(0, 0, d)) for d in range(1, 16)
    ]
    total = cs[z]
    for d in range(1, 16):
        copies[d - 1].wait_recv()
        total = total + rs[d]
    sall[k, z] = total
    sent += copies
    for d in range(1, 16):
        sent.append(send(sall.at[k, z], sall.at[k, z], as_sem.at[d], ar_sem.at[z], moved(0, 0, d)))
    for d in range(1, 16):
        oz = (z + 16 - d) % 16
        landed(sall.at[k, oz], ar_sem.at[oz], as_sem.at[0])
    sent.append(send(sall.at[k], sall.at[k], ak_sem.at[0], ak_sem.at[1], moved(0, 0, 0, 1)))
    landed(sall.at[1 - k], ak_sem.at[1], ak_sem.at[0])

    s_all = sall[...].reshape(256, 320)
    gp[...] = dot(s_all, s_all, 1, 1).reshape(16, 16, 256)
    copies = []
    for i, (a, b) in enumerate(XY):
        to_row = ((x + a) % 4) * 4 + (y + b) % 4
        copies.append(send(gp.at[to_row], grs.at[i], hs_sem.at[i], hr_sem.at[i], moved(a, b)))
    total = gp[row]
    for i in range(15):
        copies[i].wait_recv()
        total = total + grs[i]
    gall2[row] = total
    sent += copies
    for i, (a, b) in enumerate(XY):
        sent.append(send(gall2.at[row], gall2.at[row], ts_sem.at[i], tr_sem.at[row], moved(a, b)))
    for a, b in XY:
        owner = ((x + 4 - a) % 4) * 4 + (y + 4 - b) % 4
        landed(gall2.at[owner], tr_sem.at[owner], ts_sem.at[0])

    orthonormal(gall2[...].reshape(256, 256), s_all, bt_ref, ah)
    part[...] = dot(bt_ref[...], acc[...], 1, 0).reshape(16, 16, 800)

    copies = []
    for i, (a, b) in enumerate(XY):
        to_row = ((x + a) % 4) * 4 + (y + b) % 4
        copies.append(send(part.at[to_row], brs.at[i], bs_sem.at[i], br_sem.at[i], moved(a, b)))
    total = part[row]
    for i in range(15):
        copies[i].wait_recv()
        total = total + brs[i]
    sent += copies
    rall[row] = total
    diagonal = lax.broadcasted_iota(jnp.int32, (16, 128), 0) == lax.broadcasted_iota(jnp.int32, (16, 128), 1)
    squares = jnp.sum(total * total, axis=1, keepdims=True)
    sq[...] = jnp.sum(jnp.where(diagonal, squares, 0.0), axis=0, keepdims=True)
    c = send(sq, sq2, qp_sem.at[0], qp_sem.at[1], moved(0, 0, 0, 1))
    for i, (a, b) in enumerate(XY):
        sent.append(send(rall.at[row], rall.at[row], cs_sem.at[i], cr_sem.at[row], moved(a, b)))
    c.wait()
    sq[...] = sq[...] + sq2[...]
    copies = [send(sq, sqs.at[d], qs_sem.at[d], qr_sem.at[d], moved(0, 0, d)) for d in range(1, 16)]
    total = sq[...]
    for d in range(1, 16):
        copies[d - 1].wait_recv()
        total = total + sqs[d]
    sent += copies
    sqall[row] = total
    for i, (a, b) in enumerate(XY):
        sent.append(send(sqall.at[row], sqall.at[row], us_sem.at[i], ur_sem.at[row], moved(a, b)))
    for a, b in XY:
        owner = ((x + 4 - a) % 4) * 4 + (y + 4 - b) % 4
        landed(rall.at[owner], cr_sem.at[owner], cs_sem.at[0])
    right_out[...] = rall[...].reshape(256, 800)
    for a, b in XY:
        owner = ((x + 4 - a) % 4) * 4 + (y + 4 - b) % 4
        landed(sqall.at[owner], ur_sem.at[owner], us_sem.at[0])
    squares = jnp.sum(jnp.where(diagonal[None], sqall[...], 0.0), axis=2, keepdims=True)
    squares_out[...] = jnp.broadcast_to(squares.reshape(256, 1), (256, 128))
    for c in sent:
        c.wait_send()


def wide(column):
    return jnp.broadcast_to(column, (8, 128))


def factor_64(tile, parity):
    sub = lax.broadcasted_iota(jnp.int32, (8, 128), 0)
    rows = [tile[8 * t : 8 * t + 8] for t in range(8)]
    for p in range(8):
        first = 64 * parity + 8 * p
        col = {t: [wide(rows[t][:, first + j : first + j + 1]) for j in range(8)] for t in range(p, 8)}
        pivots = jnp.ones((8, 128), f32)
        for j in range(8):
            b = {i: wide(col[p][j][i : i + 1]) for i in range(j, 8)}
            inverse = 1.0 / b[j]
            pivots = jnp.where(sub == j, b[j], pivots)
            line = wide(rows[p][j : j + 1])
            for t in range(p, 8):
                factor = col[t][j] * inverse
                if t == p:
                    factor = jnp.where(sub > j, factor, 0.0)
                for i in range(j + 1, 8):
                    col[t][i] = col[t][i] - factor * b[i]
                rows[t] = rows[t] - factor * line
        rows[p] = rows[p] * lax.rsqrt(pivots)
    return jnp.concatenate(rows, axis=0)


def orthonormal(gram, sketch, bt_ref, ah):
    ah[:, 0:256] = gram
    ah[:, 256:576] = sketch
    lane = lax.broadcasted_iota(jnp.int32, (64, 128), 1)
    line = lax.broadcasted_iota(jnp.int32, (64, 128), 0)
    for b in range(4):
        parity, low = b % 2, 64 * b
        own = (lane // 64) == parity
        unit = jnp.where(lane == line + 64 * (1 - parity), 1.0, 0.0)
        tile = jnp.where(own, ah[low : low + 64, 128 * (b // 2) : 128 * (b // 2) + 128], unit)
        inverse = jnp.where(own, 0.0, factor_64(tile, parity))
        first = 128 * ((b + 1) // 2)
        block = ah[low : low + 64, first:576]
        upper = dot(inverse, jnp.concatenate([block, block], axis=0), 1, 0)
        bt_ref[low : low + 64, :] = upper[:, 256 - first :]
        if b < 3:
            change = dot(upper[:, : 256 - first], upper, 0, 0)
            ah[low + 64 : 256, first:576] = ah[low + 64 : 256, first:576] - change[low + 64 - first :, :]


def update_kernel(w_ref, moment_ref, bt_ref, right_ref, squares_ref, w_out, m_out, f_out):
    scale = lax.rsqrt(squares_ref[...][:, :1] / N + tiny_eps)
    basis = bt_ref[...].T
    right = right_ref[...]
    m_out[...] = moment_ref[...] - (1.0 - mix_rate) * dot(basis, right, 1, 0)
    factor = right * scale
    f_out[...] = factor.T
    w_out[...] = w_ref[...].astype(f32) * (1.0 - step_rate * weight_decay) - step_rate * math.sqrt(
        M / RANK
    ) * dot(basis, factor, 1, 0)


def vmem(count):
    return [pl.BlockSpec(memory_space=pltpu.VMEM)] * count


def shape(*dims):
    return jax.ShapeDtypeStruct(dims, f32)


def on_device(inputs, out_grads, weights, momentum, right_factor):
    dma = pltpu.SemaphoreType.DMA
    moment, basis_t, right, squares = pl.pallas_call(
        step_kernel,
        name="step",
        out_shape=(shape(320, 800), shape(256, 320), shape(256, 800), shape(256, 128)),
        in_specs=vmem(4),
        out_specs=tuple(vmem(4)),
        scratch_shapes=[
            pltpu.VMEM((16, 128, 800), bf16),
            pltpu.VMEM((2, 16, 64, 320), bf16),
            pltpu.VMEM((256, 800), f32),
            pltpu.VMEM((320, 800), f32),
            pltpu.VMEM((2, 16, 8, 320), f32),
            pltpu.VMEM((16, 8, 320), f32),
            pltpu.VMEM((16, 8, 320), f32),
            pltpu.VMEM((16, 8, 320), f32),
            pltpu.VMEM((2, 16, 8, 320), f32),
            pltpu.VMEM((16, 16, 256), f32),
            pltpu.VMEM((15, 16, 256), f32),
            pltpu.VMEM((16, 16, 256), f32),
            pltpu.VMEM((256, 576), f32),
            pltpu.VMEM((16, 16, 800), f32),
            pltpu.VMEM((15, 16, 800), f32),
            pltpu.VMEM((16, 16, 800), f32),
            pltpu.VMEM((1, 128), f32),
            pltpu.VMEM((1, 128), f32),
            pltpu.VMEM((16, 1, 128), f32),
            pltpu.VMEM((16, 1, 128), f32),
            dma((2,)), dma((30,)), dma((16,)), dma((16,)), dma((15,)), dma((16,)), dma((1,)), dma((1,)),
            dma((2,)), dma((16,)), dma((16,)), dma((16,)), dma((16,)), dma((2,)), dma((15,)), dma((15,)),
            dma((15,)), dma((16,)),
            dma((15,)), dma((15,)), dma((15,)), dma((16,)), dma((2,)), dma((16,)), dma((16,)), dma((15,)), dma((16,)),
        ],
        compiler_params=pltpu.CompilerParams(collective_id=0, has_side_effects=True, vmem_limit_bytes=VMEM_LIMIT),
    )(inputs, out_grads, momentum, right_factor)
    return tuple(
        pl.pallas_call(
            update_kernel,
            name="updates",
            out_shape=(shape(320, 800), shape(320, 800), shape(800, 256)),
            in_specs=vmem(5),
            out_specs=tuple(vmem(3)),
            compiler_params=pltpu.CompilerParams(vmem_limit_bytes=VMEM_LIMIT),
        )(weights, moment, basis_t, right, squares)
    )


def solution(mesh):
    return jax.shard_map(
        on_device,
        mesh=mesh,
        in_specs=(P("row", "col"), P("col", "row"), P("row", "col"), P("row", "col"), P("col", None)),
        out_specs=(P("row", "col"), P("row", "col"), P("col", None)),
        check_vma=False,
    )
```

```python
import functools
import math

import jax
import jax.numpy as jnp
from jax import lax
from jax.experimental import pallas as pl
from jax.experimental.pallas import tpu as pltpu
from jax.sharding import PartitionSpec as P

M = 5120
N = 25600
RANK = 256
TOKENS = 2048

mix_rate = 0.95
step_rate = 0.3
weight_decay = 0.1
tiny_eps = 1e-06
highest = lax.Precision.HIGHEST
MESH = pl.DeviceIdType.MESH
f32 = jnp.float32
bf16 = jnp.bfloat16
VMEM_LIMIT = 56 * 2**20
XY = [(a, b) for a in range(4) for b in range(4) if (a, b) != (0, 0)]


def place():
    r = lax.axis_index("row")
    c = lax.axis_index("col")
    return r // 4, r % 4, c // 2, c % 2


def at(x, y, z, k):
    return (x * 4 + y, z * 2 + k)


def moved(dx=0, dy=0, dz=0, dk=0):
    x, y, z, k = place()
    return at((x + dx) % 4, (y + dy) % 4, (z + dz) % 16, (k + dk) % 2)


def greet(offsets):
    barrier = pltpu.get_barrier_semaphore()
    for o in offsets:
        pl.semaphore_signal(barrier, inc=1, device_id=moved(*o), device_id_type=MESH)
    return lambda: pl.semaphore_wait(barrier, len(offsets))


def send(src, dst, send_sem, recv_sem, to):
    copy = pltpu.make_async_remote_copy(
        src_ref=src, dst_ref=dst, send_sem=send_sem, recv_sem=recv_sem, device_id=to, device_id_type=MESH
    )
    copy.start()
    return copy


def landed(dst, recv_sem, send_sem):
    pltpu.make_async_remote_copy(
        src_ref=dst, dst_ref=dst, send_sem=send_sem, recv_sem=recv_sem, device_id=moved(0, 0, 0, 1), device_id_type=MESH
    ).wait_recv()


def dot(a, b, ca, cb):
    return lax.dot_general(a, b, (((ca,), (cb,)), ((), ())), precision=highest, preferred_element_type=f32)


def dot_bf16(a, b, ca, cb):
    return lax.dot_general(a, b, (((ca,), (cb,)), ((), ())), preferred_element_type=f32)


NEAR_Z = (1, 15, 2, 14, 3, 13, 4, 12, 5, 11, 6, 10, 7, 9, 8)


def halves(value):
    high = value.astype(bf16)
    return high, (value - high.astype(f32)).astype(bf16)


BALANCED = [(1, 0), (0, 1), (3, 0), (0, 3), (1, 1), (3, 3), (1, 3), (3, 1), (2, 0), (0, 2), (1, 2), (2, 1), (3, 2), (2, 3), (2, 2)]


def step_kernel(
    x_ref, g_ref, m_ref, r_ref,
    moment_ref, high_ref, low_ref, right_out, squares_out,
    xall, gall, rt, acc, sp, pair, cs, rs, sall, gp, grs, gall2, ah, bt,
    part, brs, rall, sq, sq2, sqs, sqall,
    own_sem, xs_sem, xa_sem, xb_sem, gs_sem, gr_sem, gd_sem, gk_sem,
    p_sem, zs_sem, zr_sem, as_sem, ar_sem, aks_sem, akr_sem, hs_sem, hr_sem, ts_sem, tr_sem,
    bs_sem, br_sem, cs_sem, cr_sem, qp_sem, qs_sem, qr_sem, us_sem, ur_sem,
):
    x, y, z, k = place()
    row = x * 4 + y
    ready = greet(
        [(0, 0, d, 0) for d in NEAR_Z[::-1]]
        + [(a, b, 0, 0) for a, b in XY[::-1]]
        + [(0, 0, 0, 1)]
    )
    own_x = pltpu.make_async_copy(x_ref, xall.at[row], own_sem.at[0])
    own_g = pltpu.make_async_copy(g_ref, gall.at[z, k], own_sem.at[1])
    own_x.start()
    own_g.start()
    rt[...] = r_ref[...].T
    own_x.wait()
    own_g.wait()
    ready()

    sent = []
    number = 0
    gnum = 0

    def half(which, owner):
        return xall.at[owner, pl.ds(400 * which, 400)]

    def pass_on(which, owner, along_x, ds):
        nonlocal number
        sem = xb_sem if which else xa_sem
        for d in ds:
            to = moved(d, 0) if along_x else moved(0, d)
            sent.append(send(half(which, owner), half(which, owner), xs_sem.at[number], sem.at[owner], to))
            number += 1

    def pass_g(owner, ds):
        nonlocal gnum
        for d in ds:
            sent.append(
                send(gall.at[owner, k], gall.at[owner, k], gs_sem.at[gnum], gr_sem.at[owner], moved(0, 0, d))
            )
            gnum += 1

    def cross_g(owner):
        sent.append(send(gall.at[owner, k], gall.at[owner, k], gd_sem.at[owner], gk_sem.at[owner], moved(0, 0, 0, 1)))

    pass_g(z, (8, 4, 12))
    for d in (1, 3, 2):
        pass_on(0, row, True, (d,))
        pass_on(1, row, False, (d,))
    pass_g(z, (1, 15, 2))
    cross_g(z)
    for d in (1, 3, 2):
        pass_on(0, row, False, (d,))
        pass_on(1, row, True, (d,))
    for d in (1, 3, 2):
        ox = ((x + 4 - d) % 4) * 4 + y
        oy = x * 4 + (y + 4 - d) % 4
        landed(half(0, ox), xa_sem.at[ox], xs_sem.at[0])
        landed(half(1, oy), xb_sem.at[oy], xs_sem.at[0])
        for e in (1, 3, 2):
            pass_on(0, ox, False, (e,))
            pass_on(1, oy, True, (e,))
    for d in (4, 12, 8):
        oz = (z + 16 - d) % 16
        landed(gall.at[oz, k], gr_sem.at[oz], gs_sem.at[0])
        pass_g(oz, (1, 15, 2))
        cross_g(oz)
    for a in (0, 4, 12, 8):
        for d in (1, 15, 2):
            oz = (z + 32 - d - a) % 16
            landed(gall.at[oz, k], gr_sem.at[oz], gs_sem.at[0])
            cross_g(oz)
    for i in range(16):
        landed(gall.at[i, 1 - k], gk_sem.at[i], gd_sem.at[0])
    for a, b in XY:
        owner = ((x + 4 - a) % 4) * 4 + (y + 4 - b) % 4
        if b != 0:
            landed(half(0, owner), xa_sem.at[owner], xs_sem.at[0])
        if a != 0:
            landed(half(1, owner), xb_sem.at[owner], xs_sem.at[0])

    columns = jnp.concatenate([xall[i] for i in range(16)], axis=1)
    acc[...] = m_ref[...] + dot_bf16(gall[...].reshape(2048, 320), columns, 0, 1)
    sp[...] = dot(rt[...], acc[...], 1, 1).reshape(2, 16, 8, 320)

    c = send(sp.at[1 - k], pair, p_sem.at[0], p_sem.at[1], moved(0, 0, 0, 1))
    moment_ref[...] = acc[...]
    c.wait()
    cs[...] = sp[k] + pair[...]
    copies = [
        send(cs.at[(z + d) % 16], rs.at[d], zs_sem.at[d], zr_sem.at[d], moved(0, 0, d)) for d in NEAR_Z[::-1]
    ]
    total = cs[z]
    for i in range(15):
        copies[14 - i].wait_recv()
        total = total + rs[NEAR_Z[i]]
    sent += copies
    sall[k, z] = total
    for d in NEAR_Z[::-1]:
        sent.append(send(sall.at[k, z], sall.at[k, z], as_sem.at[d], ar_sem.at[z], moved(0, 0, d)))
    sent.append(send(sall.at[k, z], sall.at[k, z], aks_sem.at[z], akr_sem.at[z], moved(0, 0, 0, 1)))
    for d in NEAR_Z:
        oz = (z + 16 - d) % 16
        landed(sall.at[k, oz], ar_sem.at[oz], as_sem.at[0])
        sent.append(send(sall.at[k, oz], sall.at[k, oz], aks_sem.at[oz], akr_sem.at[oz], moved(0, 0, 0, 1)))
    for i in range(16):
        landed(sall.at[1 - k, i], akr_sem.at[i], aks_sem.at[0])

    s_all = sall[...].reshape(256, 320)
    gp[...] = dot(s_all, s_all, 1, 1).reshape(16, 16, 256)
    copies = []
    for i, (a, b) in enumerate(XY):
        to_row = ((x + a) % 4) * 4 + (y + b) % 4
        copies.append(send(gp.at[to_row], grs.at[i], hs_sem.at[i], hr_sem.at[i], moved(a, b)))
    total = gp[row]
    for i in range(15):
        copies[i].wait_recv()
        total = total + grs[i]
    gall2[row] = total
    sent += copies
    for i, (a, b) in enumerate(XY):
        sent.append(send(gall2.at[row], gall2.at[row], ts_sem.at[i], tr_sem.at[row], moved(a, b)))
    for a, b in XY:
        owner = ((x + 4 - a) % 4) * 4 + (y + 4 - b) % 4
        landed(gall2.at[owner], tr_sem.at[owner], ts_sem.at[0])

    ah[:, 0:256] = gall2[...].reshape(256, 256)
    ah[:, 256:576] = s_all
    right_copies = []
    for h in range(2):
        orthonormal((2 * h, 2 * h + 1), bt, ah)
        part[h] = dot(bt[128 * h : 128 * h + 128, :], acc[...], 1, 0).reshape(16, 8, 800)
        right_copies.append([])
        for i, (a, b) in enumerate(BALANCED):
            to_row = ((x + a) % 4) * 4 + (y + b) % 4
            right_copies[h].append(
                send(part.at[h, to_row], brs.at[h, i], bs_sem.at[h, i], br_sem.at[h, i], moved(a, b))
            )
    sums = []
    for h in range(2):
        total = part[h, row]
        for i in range(15):
            right_copies[h][i].wait_recv()
            total = total + brs[h, i]
        sent += right_copies[h]
        rall[h, row] = total
        sums.append(jnp.sum(total * total, axis=1, keepdims=True))
        if h == 1:
            diagonal = lax.broadcasted_iota(jnp.int32, (16, 128), 0) == lax.broadcasted_iota(jnp.int32, (16, 128), 1)
            squares = jnp.concatenate(sums, axis=0)
            sq[...] = jnp.sum(jnp.where(diagonal, squares, 0.0), axis=0, keepdims=True)
            c = send(sq, sq2, qp_sem.at[0], qp_sem.at[1], moved(0, 0, 0, 1))
        for i, (a, b) in enumerate(BALANCED):
            sent.append(send(rall.at[h, row], rall.at[h, row], cs_sem.at[h, i], cr_sem.at[h, row], moved(a, b)))
    c.wait()
    sq[...] = sq[...] + sq2[...]
    copies = [send(sq, sqs.at[d], qs_sem.at[d], qr_sem.at[d], moved(0, 0, d)) for d in NEAR_Z[::-1]]
    high_ref[...], low_ref[...] = halves(bt[...].T)
    total = sq[...]
    for i in range(15):
        copies[14 - i].wait_recv()
        total = total + sqs[NEAR_Z[i]]
    sent += copies
    sqall[row] = total
    for i, (a, b) in enumerate(BALANCED):
        sent.append(send(sqall.at[row], sqall.at[row], us_sem.at[i], ur_sem.at[row], moved(a, b)))
    for h in range(2):
        for a, b in XY:
            owner = ((x + 4 - a) % 4) * 4 + (y + 4 - b) % 4
            landed(rall.at[h, owner], cr_sem.at[h, owner], cs_sem.at[0, 0])
        right_out[128 * h : 128 * h + 128, :] = rall[h].reshape(128, 800)
    for a, b in XY:
        owner = ((x + 4 - a) % 4) * 4 + (y + 4 - b) % 4
        landed(sqall.at[owner], ur_sem.at[owner], us_sem.at[0])
    lane = lax.broadcasted_iota(jnp.int32, (16, 8, 128), 2)
    line = lax.broadcasted_iota(jnp.int32, (16, 8, 128), 1)
    rows = jnp.broadcast_to(sqall[...], (16, 8, 128))
    for h in range(2):
        squares = jnp.sum(jnp.where(lane == line + 8 * h, rows, 0.0), axis=2, keepdims=True)
        squares_out[128 * h : 128 * h + 128, :] = jnp.broadcast_to(squares.reshape(128, 1), (128, 128))
    for c in sent:
        c.wait_send()


def wide(column):
    return jnp.broadcast_to(column, (8, 128))


def factor_64(tile, parity):
    sub = lax.broadcasted_iota(jnp.int32, (8, 128), 0)
    rows = [tile[8 * t : 8 * t + 8] for t in range(8)]
    for p in range(8):
        first = 64 * parity + 8 * p
        col = {t: [wide(rows[t][:, first + j : first + j + 1]) for j in range(8)] for t in range(p, 8)}
        pivots = jnp.ones((8, 128), f32)
        for j in range(8):
            b = {i: wide(col[p][j][i : i + 1]) for i in range(j, 8)}
            inverse = 1.0 / b[j]
            pivots = jnp.where(sub == j, b[j], pivots)
            line = wide(rows[p][j : j + 1])
            for t in range(p, 8):
                factor = col[t][j] * inverse
                if t == p:
                    factor = jnp.where(sub > j, factor, 0.0)
                for i in range(j + 1, 8):
                    col[t][i] = col[t][i] - factor * b[i]
                rows[t] = rows[t] - factor * line
        rows[p] = rows[p] * lax.rsqrt(pivots)
    return jnp.concatenate(rows, axis=0)


def orthonormal(blocks, bt_ref, ah):
    lane = lax.broadcasted_iota(jnp.int32, (64, 128), 1)
    line = lax.broadcasted_iota(jnp.int32, (64, 128), 0)
    for b in blocks:
        parity, low = b % 2, 64 * b
        own = (lane // 64) == parity
        unit = jnp.where(lane == line + 64 * (1 - parity), 1.0, 0.0)
        tile = jnp.where(own, ah[low : low + 64, 128 * (b // 2) : 128 * (b // 2) + 128], unit)
        inverse = jnp.where(own, 0.0, factor_64(tile, parity))
        first = 128 * ((b + 1) // 2)
        block = ah[low : low + 64, first:576]
        upper = dot(inverse, jnp.concatenate([block, block], axis=0), 1, 0)
        bt_ref[low : low + 64, :] = upper[:, 256 - first :]
        if b < 3:
            change = dot(upper[:, : 256 - first], upper, 0, 0)
            ah[low + 64 : 256, first:576] = ah[low + 64 : 256, first:576] - change[low + 64 - first :, :]


def update_kernel(w_ref, moment_ref, high_ref, low_ref, right_ref, squares_ref, w_out, m_out, f_out, terms):
    @pl.when(pl.program_id(0) == 0)
    def _():
        right = right_ref[...]
        factor = right * lax.rsqrt(squares_ref[...][:, :1] / N + tiny_eps)
        f_out[...] = factor.T
        terms[0], terms[1] = halves(right)
        terms[2], terms[3] = halves(factor)

    high, low = high_ref[...], low_ref[...]

    def product(first, second):
        rest = dot_bf16(high, terms[second], 1, 0) + dot_bf16(low, terms[first], 1, 0)
        return dot_bf16(high, terms[first], 1, 0) + rest

    m_out[...] = moment_ref[...] - (1.0 - mix_rate) * product(0, 1)
    w_out[...] = w_ref[...].astype(f32) * (1.0 - step_rate * weight_decay) - step_rate * math.sqrt(
        M / RANK
    ) * product(2, 3)


def vmem(count):
    return [pl.BlockSpec(memory_space=pltpu.VMEM)] * count


def shape(*dims):
    return jax.ShapeDtypeStruct(dims, f32)


def on_device(inputs, out_grads, weights, momentum, right_factor):
    dma = pltpu.SemaphoreType.DMA
    moment, high, low, right, squares = pl.pallas_call(
        step_kernel,
        name="step",
        out_shape=(
            shape(320, 800),
            jax.ShapeDtypeStruct((320, 256), bf16),
            jax.ShapeDtypeStruct((320, 256), bf16),
            shape(256, 800),
            shape(256, 128),
        ),
        in_specs=vmem(4),
        out_specs=tuple(vmem(5)),
        scratch_shapes=[
            pltpu.VMEM((16, 800, 128), bf16),
            pltpu.VMEM((16, 2, 64, 320), bf16),
            pltpu.VMEM((256, 800), f32),
            pltpu.VMEM((320, 800), f32),
            pltpu.VMEM((2, 16, 8, 320), f32),
            pltpu.VMEM((16, 8, 320), f32),
            pltpu.VMEM((16, 8, 320), f32),
            pltpu.VMEM((16, 8, 320), f32),
            pltpu.VMEM((2, 16, 8, 320), f32),
            pltpu.VMEM((16, 16, 256), f32),
            pltpu.VMEM((15, 16, 256), f32),
            pltpu.VMEM((16, 16, 256), f32),
            pltpu.VMEM((256, 576), f32),
            pltpu.VMEM((256, 320), f32),
            pltpu.VMEM((2, 16, 8, 800), f32),
            pltpu.VMEM((2, 15, 8, 800), f32),
            pltpu.VMEM((2, 16, 8, 800), f32),
            pltpu.VMEM((1, 128), f32),
            pltpu.VMEM((1, 128), f32),
            pltpu.VMEM((16, 1, 128), f32),
            pltpu.VMEM((16, 1, 128), f32),
            dma((2,)), dma((30,)), dma((16,)), dma((16,)), dma((18,)), dma((16,)), dma((16,)), dma((16,)),
            dma((2,)), dma((16,)), dma((16,)), dma((16,)), dma((16,)), dma((16,)), dma((16,)),
            dma((15,)), dma((15,)), dma((15,)), dma((16,)),
            dma((2, 15)), dma((2, 15)), dma((2, 15)), dma((2, 16)),
            dma((2,)), dma((16,)), dma((16,)), dma((15,)), dma((16,)),
        ],
        compiler_params=pltpu.CompilerParams(collective_id=0, has_side_effects=True, vmem_limit_bytes=VMEM_LIMIT),
    )(inputs.T, out_grads, momentum, right_factor)
    lines, whole = (lambda i: (i, 0)), (lambda i: (0, 0))
    return tuple(
        pl.pallas_call(
            update_kernel,
            name="updates",
            grid=(4,),
            out_shape=(shape(320, 800), shape(320, 800), shape(800, 256)),
            in_specs=[
                pl.BlockSpec((80, 800), lines),
                pl.BlockSpec((80, 800), lines),
                pl.BlockSpec((80, 256), lines),
                pl.BlockSpec((80, 256), lines),
                pl.BlockSpec((256, 800), whole),
                pl.BlockSpec((256, 128), whole),
            ],
            out_specs=(
                pl.BlockSpec((80, 800), lines),
                pl.BlockSpec((80, 800), lines),
                pl.BlockSpec((800, 256), whole),
            ),
            scratch_shapes=[pltpu.VMEM((4, 256, 800), bf16)],
            compiler_params=pltpu.CompilerParams(vmem_limit_bytes=VMEM_LIMIT),
        )(weights, moment, high, low, right, squares)
    )


def solution(mesh):
    return jax.shard_map(
        on_device,
        mesh=mesh,
        in_specs=(P("row", "col"), P("col", "row"), P("row", "col"), P("row", "col"), P("col", None)),
        out_specs=(P("row", "col"), P("row", "col"), P("col", None)),
        check_vma=False,
    )
```

```python
import functools
import math

import jax
import jax.numpy as jnp
from jax import lax
from jax.experimental import pallas as pl
from jax.experimental.pallas import tpu as pltpu
from jax.sharding import PartitionSpec as P

M = 5120
N = 25600
RANK = 256
TOKENS = 2048

mix_rate = 0.95
step_rate = 0.3
weight_decay = 0.1
tiny_eps = 1e-06
highest = lax.Precision.HIGHEST
MESH = pl.DeviceIdType.MESH
f32 = jnp.float32
bf16 = jnp.bfloat16
VMEM_LIMIT = 56 * 2**20
XY = [(a, b) for a in range(4) for b in range(4) if (a, b) != (0, 0)]


def place():
    r = lax.axis_index("row")
    c = lax.axis_index("col")
    return r // 4, r % 4, c // 2, c % 2


def at(x, y, z, k):
    return (x * 4 + y, z * 2 + k)


def moved(dx=0, dy=0, dz=0, dk=0):
    x, y, z, k = place()
    return at((x + dx) % 4, (y + dy) % 4, (z + dz) % 16, (k + dk) % 2)


def greet(offsets):
    barrier = pltpu.get_barrier_semaphore()
    for o in offsets:
        pl.semaphore_signal(barrier, inc=1, device_id=moved(*o), device_id_type=MESH)
    return lambda: pl.semaphore_wait(barrier, len(offsets))


def send(src, dst, send_sem, recv_sem, to):
    copy = pltpu.make_async_remote_copy(
        src_ref=src, dst_ref=dst, send_sem=send_sem, recv_sem=recv_sem, device_id=to, device_id_type=MESH
    )
    copy.start()
    return copy


def landed(dst, recv_sem, send_sem):
    pltpu.make_async_remote_copy(
        src_ref=dst, dst_ref=dst, send_sem=send_sem, recv_sem=recv_sem, device_id=moved(0, 0, 0, 1), device_id_type=MESH
    ).wait_recv()


def dot(a, b, ca, cb):
    return lax.dot_general(a, b, (((ca,), (cb,)), ((), ())), precision=highest, preferred_element_type=f32)


def dot_bf16(a, b, ca, cb):
    return lax.dot_general(a, b, (((ca,), (cb,)), ((), ())), preferred_element_type=f32)


NEAR_Z = (1, 15, 2, 14, 3, 13, 4, 12, 5, 11, 6, 10, 7, 9, 8)


def halves(value):
    high = value.astype(bf16)
    return high, (value - high.astype(f32)).astype(bf16)


BALANCED = [(1, 0), (0, 1), (3, 0), (0, 3), (1, 1), (3, 3), (1, 3), (3, 1), (2, 0), (0, 2), (1, 2), (2, 1), (3, 2), (2, 3), (2, 2)]


def step_kernel(
    x_ref, g_ref, m_ref, r_ref,
    moment_ref, basis_out, high_ref, low_ref, right_out, squares_out,
    xall, gall, rt, acc, sp, pair, cs, rs, sall, gp, grs, gall2, ah,
    part, brs, rall, sq, sq2, sqs,
    own_sem, xs_sem, xa_sem, xb_sem, gs_sem, gr_sem, gd_sem, gk_sem,
    p_sem, zs_sem, zr_sem, as_sem, ar_sem, aks_sem, akr_sem, hs_sem, hr_sem, ts_sem, tr_sem,
    bs_sem, br_sem, cs_sem, cr_sem, qp_sem, qs_sem, qr_sem,
):
    x, y, z, k = place()
    row = x * 4 + y
    ready = greet(
        [(0, 0, d, 0) for d in NEAR_Z[::-1]]
        + [(a, b, 0, 0) for a, b in XY[::-1]]
        + [(0, 0, 0, 1)]
    )
    own_x = pltpu.make_async_copy(x_ref, xall.at[row], own_sem.at[0])
    own_g = pltpu.make_async_copy(g_ref, gall.at[z, k], own_sem.at[1])
    own_m = pltpu.make_async_copy(m_ref, acc, own_sem.at[2])
    own_x.start()
    own_g.start()
    own_m.start()
    rt[...] = r_ref[...].T
    own_x.wait()
    own_g.wait()
    ready()

    sent = []
    number = 0
    gnum = 0

    def half(which, owner):
        return xall.at[owner, pl.ds(400 * which, 400)]

    def pass_on(which, owner, along_x, ds):
        nonlocal number
        sem = xb_sem if which else xa_sem
        for d in ds:
            to = moved(d, 0) if along_x else moved(0, d)
            sent.append(send(half(which, owner), half(which, owner), xs_sem.at[number], sem.at[owner], to))
            number += 1

    def pass_g(owner, ds):
        nonlocal gnum
        for d in ds:
            sent.append(
                send(gall.at[owner, k], gall.at[owner, k], gs_sem.at[gnum], gr_sem.at[owner], moved(0, 0, d))
            )
            gnum += 1

    def cross_g(owner):
        sent.append(send(gall.at[owner, k], gall.at[owner, k], gd_sem.at[owner], gk_sem.at[owner], moved(0, 0, 0, 1)))

    pass_g(z, (8, 4, 12))
    for d in (1, 3, 2):
        pass_on(0, row, True, (d,))
        pass_on(1, row, False, (d,))
    pass_g(z, (1, 15, 2))
    cross_g(z)
    for d in (1, 3, 2):
        pass_on(0, row, False, (d,))
        pass_on(1, row, True, (d,))
    for d in (1, 3, 2):
        ox = ((x + 4 - d) % 4) * 4 + y
        oy = x * 4 + (y + 4 - d) % 4
        landed(half(0, ox), xa_sem.at[ox], xs_sem.at[0])
        landed(half(1, oy), xb_sem.at[oy], xs_sem.at[0])
        for e in (1, 3, 2):
            pass_on(0, ox, False, (e,))
            pass_on(1, oy, True, (e,))
    for d in (4, 12, 8):
        oz = (z + 16 - d) % 16
        landed(gall.at[oz, k], gr_sem.at[oz], gs_sem.at[0])
        pass_g(oz, (1, 15, 2))
        cross_g(oz)
    for a in (0, 4, 12, 8):
        for d in (1, 15, 2):
            oz = (z + 32 - d - a) % 16
            landed(gall.at[oz, k], gr_sem.at[oz], gs_sem.at[0])
            cross_g(oz)
    for i in range(16):
        landed(gall.at[i, 1 - k], gk_sem.at[i], gd_sem.at[0])
    for a, b in XY:
        owner = ((x + 4 - a) % 4) * 4 + (y + 4 - b) % 4
        if b != 0:
            landed(half(0, owner), xa_sem.at[owner], xs_sem.at[0])
        if a != 0:
            landed(half(1, owner), xb_sem.at[owner], xs_sem.at[0])

    columns = jnp.concatenate([xall[i] for i in range(16)], axis=1)
    own_m.wait()
    acc[...] += dot_bf16(gall[...].reshape(2048, 320), columns, 0, 1)
    moment_copy = pltpu.make_async_copy(acc, moment_ref, own_sem.at[3])
    moment_copy.start()
    other = rt[pl.ds(pl.multiple_of(128 * (1 - k), 128), 128), :]
    sp[1 - k] = dot(other, acc[...], 1, 1).reshape(16, 8, 320)

    c = send(sp.at[1 - k], pair, p_sem.at[0], p_sem.at[1], moved(0, 0, 0, 1))
    own = rt[pl.ds(pl.multiple_of(128 * k, 128), 128), :]
    sp[k] = dot(own, acc[...], 1, 1).reshape(16, 8, 320)
    c.wait()
    cs[...] = sp[k] + pair[...]
    copies = [
        send(cs.at[(z + d) % 16], rs.at[d], zs_sem.at[d], zr_sem.at[d], moved(0, 0, d)) for d in NEAR_Z[::-1]
    ]
    total = cs[z]
    for i in range(15):
        copies[14 - i].wait_recv()
        total = total + rs[NEAR_Z[i]]
    sent += copies
    sall[k, z] = total
    for d in NEAR_Z[::-1]:
        sent.append(send(sall.at[k, z], sall.at[k, z], as_sem.at[d], ar_sem.at[z], moved(0, 0, d)))
    sent.append(send(sall.at[k, z], sall.at[k, z], aks_sem.at[z], akr_sem.at[z], moved(0, 0, 0, 1)))
    for d in NEAR_Z:
        oz = (z + 16 - d) % 16
        landed(sall.at[k, oz], ar_sem.at[oz], as_sem.at[0])
        sent.append(send(sall.at[k, oz], sall.at[k, oz], aks_sem.at[oz], akr_sem.at[oz], moved(0, 0, 0, 1)))
    for i in range(16):
        landed(sall.at[1 - k, i], akr_sem.at[i], aks_sem.at[0])

    s_all = sall[...].reshape(256, 320)
    gp[...] = dot(s_all, s_all, 1, 1).reshape(16, 16, 256)
    copies = []
    for i, (a, b) in enumerate(BALANCED):
        to_row = ((x + a) % 4) * 4 + (y + b) % 4
        copies.append(send(gp.at[to_row], grs.at[i], hs_sem.at[i], hr_sem.at[i], moved(a, b)))
    right_copies = []
    for h in range(2):
        part[h] = dot(sall[h].reshape(128, 320), acc[...], 1, 0).reshape(16, 8, 800)
        right_copies.append([])
        for i, (a, b) in enumerate(BALANCED):
            to_row = ((x + a) % 4) * 4 + (y + b) % 4
            right_copies[h].append(
                send(part.at[h, to_row], brs.at[h, i], bs_sem.at[h, i], br_sem.at[h, i], moved(a, b))
            )
    total = gp[row]
    for i in range(15):
        copies[i].wait_recv()
        total = total + grs[i]
    gall2[row] = total
    sent += copies
    for i, (a, b) in enumerate(BALANCED):
        sent.append(send(gall2.at[row], gall2.at[row], ts_sem.at[i], tr_sem.at[row], moved(a, b)))
    for h in range(2):
        total = part[h, row]
        for i in range(15):
            right_copies[h][i].wait_recv()
            total = total + brs[h, i]
        sent += right_copies[h]
        rall[h, row] = total
        for i, (a, b) in enumerate(BALANCED):
            sent.append(send(rall.at[h, row], rall.at[h, row], cs_sem.at[h, i], cr_sem.at[h, row], moved(a, b)))
    for a, b in XY:
        owner = ((x + 4 - a) % 4) * 4 + (y + 4 - b) % 4
        landed(gall2.at[owner], tr_sem.at[owner], ts_sem.at[0])

    inverse = factor_inverse(gall2[...].reshape(256, 256), ah)
    basis_out[...] = dot(inverse, s_all, 1, 0).T
    for h in range(2):
        for a, b in XY:
            owner = ((x + 4 - a) % 4) * 4 + (y + 4 - b) % 4
            landed(rall.at[h, owner], cr_sem.at[h, owner], cs_sem.at[0, 0])
    right = dot(inverse, rall[...].reshape(256, 800), 1, 0)

    diagonal = lax.broadcasted_iota(jnp.int32, (128, 128), 0) == lax.broadcasted_iota(jnp.int32, (128, 128), 1)
    squares = jnp.sum(right * right, axis=1, keepdims=True)
    for h in range(2):
        line = jnp.where(diagonal, squares[128 * h : 128 * h + 128], 0.0)
        sq[:, 128 * h : 128 * h + 128] = jnp.sum(line, axis=0, keepdims=True)
    c = send(sq, sq2, qp_sem.at[0], qp_sem.at[1], moved(0, 0, 0, 1))
    c.wait()
    sq[...] = sq[...] + sq2[...]
    copies = [send(sq, sqs.at[d], qs_sem.at[d], qr_sem.at[d], moved(0, 0, d)) for d in NEAR_Z[::-1]]
    high_ref[...], low_ref[...] = halves(right)
    right_out[...] = right.T
    total = sq[...]
    for i in range(15):
        copies[14 - i].wait_recv()
        total = total + sqs[NEAR_Z[i]]
    sent += copies
    squares_out[...] = total
    moment_copy.wait()
    for c in sent:
        c.wait_send()


def wide(column):
    return jnp.broadcast_to(column, (8, 128))


def factor_64(tile, parity):
    sub = lax.broadcasted_iota(jnp.int32, (8, 128), 0)
    rows = [tile[8 * t : 8 * t + 8] for t in range(8)]
    for p in range(8):
        first = 64 * parity + 8 * p
        col = {t: [wide(rows[t][:, first + j : first + j + 1]) for j in range(8)] for t in range(p, 8)}
        pivots = jnp.ones((8, 128), f32)
        for j in range(8):
            b = {i: wide(col[p][j][i : i + 1]) for i in range(j, 8)}
            inverse = 1.0 / b[j]
            pivots = jnp.where(sub == j, b[j], pivots)
            line = wide(rows[p][j : j + 1])
            for t in range(p, 8):
                factor = col[t][j] * inverse
                for i in range(j + 1, 8):
                    col[t][i] = col[t][i] - factor * b[i]
                if t == p:
                    factor = jnp.where(sub > j, factor, 0.0)
                rows[t] = rows[t] - factor * line
        rows[p] = rows[p] * lax.rsqrt(pivots)
    return jnp.concatenate(rows, axis=0)


def factor_inverse(gram, ah):
    ah[:, 0:256] = gram
    lines = lax.broadcasted_iota(jnp.int32, (256, 256), 0)
    ah[:, 256:512] = jnp.where(lines == lax.broadcasted_iota(jnp.int32, (256, 256), 1), 1.0, 0.0)
    done = []
    lane = lax.broadcasted_iota(jnp.int32, (64, 128), 1)
    line = lax.broadcasted_iota(jnp.int32, (64, 128), 0)
    for b in range(4):
        parity, low = b % 2, 64 * b
        own = (lane // 64) == parity
        unit = jnp.where(lane == line + 64 * (1 - parity), 1.0, 0.0)
        tile = jnp.where(own, ah[low : low + 64, 128 * (b // 2) : 128 * (b // 2) + 128], unit)
        inverse = jnp.where(own, 0.0, factor_64(tile, parity))
        first = 128 * ((b + 1) // 2)
        block = ah[low : low + 64, first:512]
        upper = dot(inverse, jnp.concatenate([block, block], axis=0), 1, 0)
        done.append(upper[:, 256 - first :])
        if b < 3:
            change = dot(upper[:, : 256 - first], upper, 0, 0)
            ah[low + 64 : 256, first:512] = ah[low + 64 : 256, first:512] - change[low + 64 - first :, :]
    return jnp.concatenate(done, axis=0)


def update_kernel(w_ref, moment_ref, basis_ref, high_ref, low_ref, right_ref, squares_ref, w_out, m_out, f_out):
    scale = lax.rsqrt(squares_ref[...] / N + tiny_eps)
    f_out[...] = right_ref[...] * scale

    def product(left):
        high, low = halves(left)
        rest = dot_bf16(high, low_ref[...], 1, 0) + dot_bf16(low, high_ref[...], 1, 0)
        return dot_bf16(high, high_ref[...], 1, 0) + rest

    basis = basis_ref[...]
    m_out[...] = moment_ref[...] - (1.0 - mix_rate) * product(basis)
    w_out[...] = w_ref[...].astype(f32) * (1.0 - step_rate * weight_decay) - step_rate * math.sqrt(
        M / RANK
    ) * product(basis * scale)


def vmem(count):
    return [pl.BlockSpec(memory_space=pltpu.VMEM)] * count


def shape(*dims):
    return jax.ShapeDtypeStruct(dims, f32)


def on_device(inputs, out_grads, weights, momentum, right_factor):
    dma = pltpu.SemaphoreType.DMA
    moment, basis, high, low, right, squares = pl.pallas_call(
        step_kernel,
        name="step",
        out_shape=(
            shape(320, 800),
            shape(320, 256),
            jax.ShapeDtypeStruct((256, 800), bf16),
            jax.ShapeDtypeStruct((256, 800), bf16),
            shape(800, 256),
            shape(1, 256),
        ),
        in_specs=vmem(2) + [pl.BlockSpec(memory_space=pl.ANY)] + vmem(1),
        out_specs=(pl.BlockSpec(memory_space=pl.ANY), *vmem(5)),
        scratch_shapes=[
            pltpu.VMEM((16, 800, 128), bf16),
            pltpu.VMEM((16, 2, 64, 320), bf16),
            pltpu.VMEM((256, 800), f32),
            pltpu.VMEM((320, 800), f32),
            pltpu.VMEM((2, 16, 8, 320), f32),
            pltpu.VMEM((16, 8, 320), f32),
            pltpu.VMEM((16, 8, 320), f32),
            pltpu.VMEM((16, 8, 320), f32),
            pltpu.VMEM((2, 16, 8, 320), f32),
            pltpu.VMEM((16, 16, 256), f32),
            pltpu.VMEM((15, 16, 256), f32),
            pltpu.VMEM((16, 16, 256), f32),
            pltpu.VMEM((256, 512), f32),
            pltpu.VMEM((2, 16, 8, 800), f32),
            pltpu.VMEM((2, 15, 8, 800), f32),
            pltpu.VMEM((2, 16, 8, 800), f32),
            pltpu.VMEM((1, 256), f32),
            pltpu.VMEM((1, 256), f32),
            pltpu.VMEM((16, 1, 256), f32),
            dma((4,)), dma((30,)), dma((16,)), dma((16,)), dma((18,)), dma((16,)), dma((16,)), dma((16,)),
            dma((2,)), dma((16,)), dma((16,)), dma((16,)), dma((16,)), dma((16,)), dma((16,)),
            dma((15,)), dma((15,)), dma((15,)), dma((16,)),
            dma((2, 15)), dma((2, 15)), dma((2, 15)), dma((2, 16)),
            dma((2,)), dma((16,)), dma((16,)),
        ],
        compiler_params=pltpu.CompilerParams(collective_id=0, has_side_effects=True, vmem_limit_bytes=VMEM_LIMIT),
    )(inputs.T, out_grads, momentum, right_factor)
    lines, whole = (lambda i: (i, 0)), (lambda i: (0, 0))
    return tuple(
        pl.pallas_call(
            update_kernel,
            name="updates",
            grid=(4,),
            out_shape=(shape(320, 800), shape(320, 800), shape(800, 256)),
            in_specs=[
                pl.BlockSpec((80, 800), lines),
                pl.BlockSpec((80, 800), lines),
                pl.BlockSpec((80, 256), lines),
                pl.BlockSpec((256, 800), whole),
                pl.BlockSpec((256, 800), whole),
                pl.BlockSpec((200, 256), lines),
                pl.BlockSpec((1, 256), whole),
            ],
            out_specs=(
                pl.BlockSpec((80, 800), lines),
                pl.BlockSpec((80, 800), lines),
                pl.BlockSpec((200, 256), lines),
            ),
            compiler_params=pltpu.CompilerParams(vmem_limit_bytes=VMEM_LIMIT),
        )(weights, moment, basis, high, low, right, squares)
    )


def solution(mesh):
    return jax.shard_map(
        on_device,
        mesh=mesh,
        in_specs=(P("row", "col"), P("col", "row"), P("row", "col"), P("row", "col"), P("col", None)),
        out_specs=(P("row", "col"), P("row", "col"), P("col", None)),
        check_vma=False,
    )
```

```python
import functools
import math

import jax
import jax.numpy as jnp
from jax import lax
from jax.experimental import pallas as pl
from jax.experimental.pallas import tpu as pltpu
from jax.sharding import PartitionSpec as P

M = 5120
N = 25600
RANK = 256
TOKENS = 2048

mix_rate = 0.95
step_rate = 0.3
weight_decay = 0.1
tiny_eps = 1e-06
highest = lax.Precision.HIGHEST
MESH = pl.DeviceIdType.MESH
f32 = jnp.float32
bf16 = jnp.bfloat16
VMEM_LIMIT = 56 * 2**20
XY = [(a, b) for a in range(4) for b in range(4) if (a, b) != (0, 0)]


def place():
    r = lax.axis_index("row")
    c = lax.axis_index("col")
    return r // 4, r % 4, c // 2, c % 2


def at(x, y, z, k):
    return (x * 4 + y, z * 2 + k)


def moved(dx=0, dy=0, dz=0, dk=0):
    x, y, z, k = place()
    return at((x + dx) % 4, (y + dy) % 4, (z + dz) % 16, (k + dk) % 2)


def greet(offsets):
    barrier = pltpu.get_barrier_semaphore()
    for o in offsets:
        pl.semaphore_signal(barrier, inc=1, device_id=moved(*o), device_id_type=MESH)
    return lambda: pl.semaphore_wait(barrier, len(offsets))


def send(src, dst, send_sem, recv_sem, to):
    copy = pltpu.make_async_remote_copy(
        src_ref=src, dst_ref=dst, send_sem=send_sem, recv_sem=recv_sem, device_id=to, device_id_type=MESH
    )
    copy.start()
    return copy


def landed(dst, recv_sem, send_sem):
    pltpu.make_async_remote_copy(
        src_ref=dst, dst_ref=dst, send_sem=send_sem, recv_sem=recv_sem, device_id=moved(0, 0, 0, 1), device_id_type=MESH
    ).wait_recv()


def dot(a, b, ca, cb):
    return lax.dot_general(a, b, (((ca,), (cb,)), ((), ())), precision=highest, preferred_element_type=f32)


def dot_bf16(a, b, ca, cb):
    return lax.dot_general(a, b, (((ca,), (cb,)), ((), ())), preferred_element_type=f32)


NEAR_Z = (1, 15, 2, 14, 3, 13, 4, 12, 5, 11, 6, 10, 7, 9, 8)


def halves(value):
    high = value.astype(bf16)
    return high, (value - high.astype(f32)).astype(bf16)


BALANCED = [(1, 0), (0, 1), (3, 0), (0, 3), (1, 1), (3, 3), (1, 3), (3, 1), (2, 0), (0, 2), (1, 2), (2, 1), (3, 2), (2, 3), (2, 2)]


def step_kernel(
    x_ref, g_ref, m_ref, r_ref,
    moment_ref, basis_out, high_ref, low_ref, right_out, squares_out,
    xall, gall, rt, acc, sp, pair, cs, rs, sall, gp, grs, gall2, ah,
    part, brs, rall, sq, sq2, sqs,
    own_sem, xs_sem, xa_sem, xb_sem, gs_sem, gr_sem, gd_sem, gk_sem,
    p_sem, zs_sem, zr_sem, as_sem, ar_sem, aks_sem, akr_sem, hs_sem, hr_sem, ts_sem, tr_sem,
    bs_sem, br_sem, cs_sem, cr_sem, qp_sem, qs_sem, qr_sem,
):
    x, y, z, k = place()
    row = x * 4 + y
    ready = greet([(d, 0, 0, 0) for d in (2, 1, 3)] + [(0, d, 0, 0) for d in (2, 1, 3)] + [(0, 0, d, 0) for d in (2, 14, 1, 15)] + [(0, 0, 0, 1)])
    own_x = pltpu.make_async_copy(x_ref, xall.at[row], own_sem.at[0])
    own_g = pltpu.make_async_copy(g_ref, gall.at[z, k], own_sem.at[1])
    own_m = pltpu.make_async_copy(m_ref, acc, own_sem.at[2])
    own_x.start()
    own_g.start()
    own_m.start()
    rt[...] = r_ref[...].T
    own_x.wait()
    own_g.wait()
    ready()

    sent = []
    number = 0
    gnum = 0

    def half(which, owner):
        return xall.at[owner, pl.ds(400 * which, 400)]

    def pass_on(which, owner, along_x, ds):
        nonlocal number
        sem = xb_sem if which else xa_sem
        for d in ds:
            to = moved(d, 0) if along_x else moved(0, d)
            sent.append(send(half(which, owner), half(which, owner), xs_sem.at[number], sem.at[owner], to))
            number += 1

    def pass_g(owner, ds):
        nonlocal gnum
        for d in ds:
            sent.append(
                send(gall.at[owner, k], gall.at[owner, k], gs_sem.at[gnum], gr_sem.at[owner], moved(0, 0, d))
            )
            gnum += 1

    def cross_g(owner):
        sent.append(send(gall.at[owner, k], gall.at[owner, k], gd_sem.at[owner], gk_sem.at[owner], moved(0, 0, 0, 1)))

    def relay_x(d):
        ox = ((x + 4 - d) % 4) * 4 + y
        oy = x * 4 + (y + 4 - d) % 4
        landed(half(0, ox), xa_sem.at[ox], xs_sem.at[0])
        landed(half(1, oy), xb_sem.at[oy], xs_sem.at[0])
        for e in (1, 3, 2):
            pass_on(0, ox, False, (e,))
            pass_on(1, oy, True, (e,))

    def take_g(owner, ds):
        landed(gall.at[owner, k], gr_sem.at[owner], gs_sem.at[0])
        pass_g(owner, ds)
        cross_g(owner)

    def relay_g(d):
        take_g((z + 16 - d) % 16, (2, 1))
        take_g((z + d) % 16, (14, 15) if d < 6 else (15,))

    pass_g(z, (2, 14, 1, 15))
    for d in (1, 3, 2):
        pass_on(0, row, True, (d,))
        pass_on(1, row, False, (d,))
    cross_g(z)
    for d in (1, 3, 2):
        pass_on(0, row, False, (d,))
        pass_on(1, row, True, (d,))
    relay_g(2)
    relay_x(1)
    relay_g(4)
    relay_x(3)
    relay_x(2)
    relay_g(6)
    for d in (1, 3, 5, 7):
        take_g((z + 16 - d) % 16, ())
        take_g((z + d) % 16, ())
    take_g((z + 8) % 16, ())
    for i in range(16):
        landed(gall.at[i, 1 - k], gk_sem.at[i], gd_sem.at[0])
    for a, b in XY:
        owner = ((x + 4 - a) % 4) * 4 + (y + 4 - b) % 4
        if b != 0:
            landed(half(0, owner), xa_sem.at[owner], xs_sem.at[0])
        if a != 0:
            landed(half(1, owner), xb_sem.at[owner], xs_sem.at[0])

    columns = jnp.concatenate([xall[i] for i in range(16)], axis=1)
    own_m.wait()
    acc[...] += dot_bf16(gall[...].reshape(2048, 320), columns, 0, 1)
    moment_copy = pltpu.make_async_copy(acc, moment_ref, own_sem.at[3])
    moment_copy.start()
    other = rt[pl.ds(pl.multiple_of(128 * (1 - k), 128), 128), :]
    sp[1 - k] = dot(other, acc[...], 1, 1).reshape(16, 8, 320)

    c = send(sp.at[1 - k], pair, p_sem.at[0], p_sem.at[1], moved(0, 0, 0, 1))
    own = rt[pl.ds(pl.multiple_of(128 * k, 128), 128), :]
    sp[k] = dot(own, acc[...], 1, 1).reshape(16, 8, 320)
    c.wait()
    cs[...] = sp[k] + pair[...]
    copies = [
        send(cs.at[(z + d) % 16], rs.at[d], zs_sem.at[d], zr_sem.at[d], moved(0, 0, d)) for d in NEAR_Z[::-1]
    ]
    total = cs[z]
    for i in range(15):
        copies[14 - i].wait_recv()
        total = total + rs[NEAR_Z[i]]
    sent += copies
    sall[k, z] = total
    for d in NEAR_Z[::-1]:
        sent.append(send(sall.at[k, z], sall.at[k, z], as_sem.at[d], ar_sem.at[z], moved(0, 0, d)))
    sent.append(send(sall.at[k, z], sall.at[k, z], aks_sem.at[z], akr_sem.at[z], moved(0, 0, 0, 1)))
    for d in NEAR_Z:
        oz = (z + 16 - d) % 16
        landed(sall.at[k, oz], ar_sem.at[oz], as_sem.at[0])
        sent.append(send(sall.at[k, oz], sall.at[k, oz], aks_sem.at[oz], akr_sem.at[oz], moved(0, 0, 0, 1)))
    for i in range(16):
        landed(sall.at[1 - k, i], akr_sem.at[i], aks_sem.at[0])

    s_all = sall[...].reshape(256, 320)
    gp[...] = dot(s_all, s_all, 1, 1).reshape(16, 16, 256)
    copies = []
    for i, (a, b) in enumerate(BALANCED):
        to_row = ((x + a) % 4) * 4 + (y + b) % 4
        copies.append(send(gp.at[to_row], grs.at[i], hs_sem.at[i], hr_sem.at[i], moved(a, b)))
    right_copies = []
    for h in range(2):
        part[h] = dot(sall[h].reshape(128, 320), acc[...], 1, 0).reshape(16, 8, 800)
        right_copies.append([])
        for i, (a, b) in enumerate(BALANCED):
            to_row = ((x + a) % 4) * 4 + (y + b) % 4
            right_copies[h].append(
                send(part.at[h, to_row], brs.at[h, i], bs_sem.at[h, i], br_sem.at[h, i], moved(a, b))
            )
    total = gp[row]
    for i in range(15):
        copies[i].wait_recv()
        total = total + grs[i]
    gall2[row] = total
    sent += copies
    for i, (a, b) in enumerate(BALANCED):
        sent.append(send(gall2.at[row], gall2.at[row], ts_sem.at[i], tr_sem.at[row], moved(a, b)))
    for h in range(2):
        total = part[h, row]
        for i in range(15):
            right_copies[h][i].wait_recv()
            total = total + brs[h, i]
        sent += right_copies[h]
        rall[h, row] = total
        for i, (a, b) in enumerate(BALANCED):
            sent.append(send(rall.at[h, row], rall.at[h, row], cs_sem.at[h, i], cr_sem.at[h, row], moved(a, b)))
    for a, b in XY:
        owner = ((x + 4 - a) % 4) * 4 + (y + 4 - b) % 4
        landed(gall2.at[owner], tr_sem.at[owner], ts_sem.at[0])

    inverse = factor_inverse(gall2[...].reshape(256, 256), ah)
    basis_out[...] = dot(inverse, s_all, 1, 0).T
    for h in range(2):
        for a, b in XY:
            owner = ((x + 4 - a) % 4) * 4 + (y + 4 - b) % 4
            landed(rall.at[h, owner], cr_sem.at[h, owner], cs_sem.at[0, 0])
    right = dot(inverse, rall[...].reshape(256, 800), 1, 0)

    diagonal = lax.broadcasted_iota(jnp.int32, (128, 128), 0) == lax.broadcasted_iota(jnp.int32, (128, 128), 1)
    squares = jnp.sum(right * right, axis=1, keepdims=True)
    for h in range(2):
        line = jnp.where(diagonal, squares[128 * h : 128 * h + 128], 0.0)
        sq[:, 128 * h : 128 * h + 128] = jnp.sum(line, axis=0, keepdims=True)
    c = send(sq, sq2, qp_sem.at[0], qp_sem.at[1], moved(0, 0, 0, 1))
    c.wait()
    sq[...] = sq[...] + sq2[...]
    copies = [send(sq, sqs.at[d], qs_sem.at[d], qr_sem.at[d], moved(0, 0, d)) for d in NEAR_Z[::-1]]
    high_ref[...], low_ref[...] = halves(right)
    right_out[...] = right.T
    total = sq[...]
    for i in range(15):
        copies[14 - i].wait_recv()
        total = total + sqs[NEAR_Z[i]]
    sent += copies
    squares_out[...] = total
    moment_copy.wait()
    for c in sent:
        c.wait_send()


def wide(column):
    return jnp.broadcast_to(column, (8, 128))


def factor_64(tile, parity):
    sub = lax.broadcasted_iota(jnp.int32, (8, 128), 0)
    rows = [tile[8 * t : 8 * t + 8] for t in range(8)]
    for p in range(8):
        first = 64 * parity + 8 * p
        col = {t: [wide(rows[t][:, first + j : first + j + 1]) for j in range(8)] for t in range(p, 8)}
        pivots = jnp.ones((8, 128), f32)
        for j in range(8):
            b = {i: wide(col[p][j][i : i + 1]) for i in range(j, 8)}
            inverse = 1.0 / b[j]
            pivots = jnp.where(sub == j, b[j], pivots)
            line = wide(rows[p][j : j + 1])
            for t in range(p, 8):
                factor = col[t][j] * inverse
                for i in range(j + 1, 8):
                    col[t][i] = col[t][i] - factor * b[i]
                if t == p:
                    factor = jnp.where(sub > j, factor, 0.0)
                rows[t] = rows[t] - factor * line
        rows[p] = rows[p] * lax.rsqrt(pivots)
    return jnp.concatenate(rows, axis=0)


def factor_inverse(gram, ah):
    ah[:, 0:256] = gram
    lines = lax.broadcasted_iota(jnp.int32, (256, 256), 0)
    ah[:, 256:512] = jnp.where(lines == lax.broadcasted_iota(jnp.int32, (256, 256), 1), 1.0, 0.0)
    done = []
    lane = lax.broadcasted_iota(jnp.int32, (64, 128), 1)
    line = lax.broadcasted_iota(jnp.int32, (64, 128), 0)
    for b in range(4):
        parity, low = b % 2, 64 * b
        own = (lane // 64) == parity
        unit = jnp.where(lane == line + 64 * (1 - parity), 1.0, 0.0)
        tile = jnp.where(own, ah[low : low + 64, 128 * (b // 2) : 128 * (b // 2) + 128], unit)
        inverse = jnp.where(own, 0.0, factor_64(tile, parity))
        first = 128 * ((b + 1) // 2)
        block = ah[low : low + 64, first:512]
        upper = dot(inverse, jnp.concatenate([block, block], axis=0), 1, 0)
        done.append(upper[:, 256 - first :])
        if b < 3:
            change = dot(upper[:, : 256 - first], upper, 0, 0)
            ah[low + 64 : 256, first:512] = ah[low + 64 : 256, first:512] - change[low + 64 - first :, :]
    return jnp.concatenate(done, axis=0)


def update_kernel(w_ref, moment_ref, basis_ref, high_ref, low_ref, right_ref, squares_ref, w_out, m_out, f_out):
    scale = lax.rsqrt(squares_ref[...] / N + tiny_eps)
    f_out[...] = right_ref[...] * scale

    def product(left):
        high, low = halves(left)
        rest = dot_bf16(high, low_ref[...], 1, 0) + dot_bf16(low, high_ref[...], 1, 0)
        return dot_bf16(high, high_ref[...], 1, 0) + rest

    basis = basis_ref[...]
    m_out[...] = moment_ref[...] - (1.0 - mix_rate) * product(basis)
    w_out[...] = w_ref[...].astype(f32) * (1.0 - step_rate * weight_decay) - step_rate * math.sqrt(
        M / RANK
    ) * product(basis * scale)


def vmem(count):
    return [pl.BlockSpec(memory_space=pltpu.VMEM)] * count


def shape(*dims):
    return jax.ShapeDtypeStruct(dims, f32)


def on_device(inputs, out_grads, weights, momentum, right_factor):
    dma = pltpu.SemaphoreType.DMA
    moment, basis, high, low, right, squares = pl.pallas_call(
        step_kernel,
        name="step",
        out_shape=(
            shape(320, 800),
            shape(320, 256),
            jax.ShapeDtypeStruct((256, 800), bf16),
            jax.ShapeDtypeStruct((256, 800), bf16),
            shape(800, 256),
            shape(1, 256),
        ),
        in_specs=vmem(2) + [pl.BlockSpec(memory_space=pl.ANY)] + vmem(1),
        out_specs=(pl.BlockSpec(memory_space=pl.ANY), *vmem(5)),
        scratch_shapes=[
            pltpu.VMEM((16, 800, 128), bf16),
            pltpu.VMEM((16, 2, 64, 320), bf16),
            pltpu.VMEM((256, 800), f32),
            pltpu.VMEM((320, 800), f32),
            pltpu.VMEM((2, 16, 8, 320), f32),
            pltpu.VMEM((16, 8, 320), f32),
            pltpu.VMEM((16, 8, 320), f32),
            pltpu.VMEM((16, 8, 320), f32),
            pltpu.VMEM((2, 16, 8, 320), f32),
            pltpu.VMEM((16, 16, 256), f32),
            pltpu.VMEM((15, 16, 256), f32),
            pltpu.VMEM((16, 16, 256), f32),
            pltpu.VMEM((256, 512), f32),
            pltpu.VMEM((2, 16, 8, 800), f32),
            pltpu.VMEM((2, 15, 8, 800), f32),
            pltpu.VMEM((2, 16, 8, 800), f32),
            pltpu.VMEM((1, 256), f32),
            pltpu.VMEM((1, 256), f32),
            pltpu.VMEM((16, 1, 256), f32),
            dma((4,)), dma((30,)), dma((16,)), dma((16,)), dma((18,)), dma((16,)), dma((16,)), dma((16,)),
            dma((2,)), dma((16,)), dma((16,)), dma((16,)), dma((16,)), dma((16,)), dma((16,)),
            dma((15,)), dma((15,)), dma((15,)), dma((16,)),
            dma((2, 15)), dma((2, 15)), dma((2, 15)), dma((2, 16)),
            dma((2,)), dma((16,)), dma((16,)),
        ],
        compiler_params=pltpu.CompilerParams(collective_id=0, has_side_effects=True, vmem_limit_bytes=VMEM_LIMIT),
    )(inputs.T, out_grads, momentum, right_factor)
    lines, whole = (lambda i: (i, 0)), (lambda i: (0, 0))
    return tuple(
        pl.pallas_call(
            update_kernel,
            name="updates",
            grid=(4,),
            out_shape=(shape(320, 800), shape(320, 800), shape(800, 256)),
            in_specs=[
                pl.BlockSpec((80, 800), lines),
                pl.BlockSpec((80, 800), lines),
                pl.BlockSpec((80, 256), lines),
                pl.BlockSpec((256, 800), whole),
                pl.BlockSpec((256, 800), whole),
                pl.BlockSpec((200, 256), lines),
                pl.BlockSpec((1, 256), whole),
            ],
            out_specs=(
                pl.BlockSpec((80, 800), lines),
                pl.BlockSpec((80, 800), lines),
                pl.BlockSpec((200, 256), lines),
            ),
            compiler_params=pltpu.CompilerParams(vmem_limit_bytes=VMEM_LIMIT),
        )(weights, moment, basis, high, low, right, squares)
    )


def solution(mesh):
    return jax.shard_map(
        on_device,
        mesh=mesh,
        in_specs=(P("row", "col"), P("col", "row"), P("row", "col"), P("row", "col"), P("col", None)),
        out_specs=(P("row", "col"), P("row", "col"), P("col", None)),
        check_vma=False,
    )
```

```python
import functools
import math

import jax
import jax.numpy as jnp
from jax import lax
from jax.experimental import pallas as pl
from jax.experimental.pallas import tpu as pltpu
from jax.sharding import PartitionSpec as P

M = 5120
N = 25600
RANK = 256
TOKENS = 2048

mix_rate = 0.95
step_rate = 0.3
weight_decay = 0.1
tiny_eps = 1e-06
highest = lax.Precision.HIGHEST
MESH = pl.DeviceIdType.MESH
f32 = jnp.float32
bf16 = jnp.bfloat16
VMEM_LIMIT = 56 * 2**20
XY = [(a, b) for a in range(4) for b in range(4) if (a, b) != (0, 0)]


def place():
    r = lax.axis_index("row")
    c = lax.axis_index("col")
    return r // 4, r % 4, c // 2, c % 2


def at(x, y, z, k):
    return (x * 4 + y, z * 2 + k)


def moved(dx=0, dy=0, dz=0, dk=0):
    x, y, z, k = place()
    return at((x + dx) % 4, (y + dy) % 4, (z + dz) % 16, (k + dk) % 2)


def greet(offsets):
    barrier = pltpu.get_barrier_semaphore()
    for o in offsets:
        pl.semaphore_signal(barrier, inc=1, device_id=moved(*o), device_id_type=MESH)
    return lambda: pl.semaphore_wait(barrier, len(offsets))


def send(src, dst, send_sem, recv_sem, to):
    copy = pltpu.make_async_remote_copy(
        src_ref=src, dst_ref=dst, send_sem=send_sem, recv_sem=recv_sem, device_id=to, device_id_type=MESH
    )
    copy.start()
    return copy


def landed(dst, recv_sem, send_sem):
    pltpu.make_async_remote_copy(
        src_ref=dst, dst_ref=dst, send_sem=send_sem, recv_sem=recv_sem, device_id=moved(0, 0, 0, 1), device_id_type=MESH
    ).wait_recv()


def dot(a, b, ca, cb):
    return lax.dot_general(a, b, (((ca,), (cb,)), ((), ())), precision=highest, preferred_element_type=f32)


def dot_bf16(a, b, ca, cb):
    return lax.dot_general(a, b, (((ca,), (cb,)), ((), ())), preferred_element_type=f32)


NEAR_Z = (1, 15, 2, 14, 3, 13, 4, 12, 5, 11, 6, 10, 7, 9, 8)


def halves(value):
    high = value.astype(bf16)
    return high, (value - high.astype(f32)).astype(bf16)


BALANCED = [(1, 0), (0, 1), (3, 0), (0, 3), (1, 1), (3, 3), (1, 3), (3, 1), (2, 0), (0, 2), (1, 2), (2, 1), (3, 2), (2, 3), (2, 2)]


def step_kernel(
    x_ref, g_ref, m_ref, r_ref,
    moment_ref, basis_out, high_ref, low_ref, right_out, squares_out,
    xall, gall, gt, rt, acc, sp, pair, cs, rs, sall, gp, grs, gall2, ah,
    part, brs, rall, sq, sq2, sqs,
    own_sem, xs_sem, xa_sem, xb_sem, gs_sem, gr_sem, gd_sem, gk_sem,
    p_sem, zs_sem, zr_sem, as_sem, ar_sem, aks_sem, akr_sem, hs_sem, hr_sem, ts_sem, tr_sem,
    bs_sem, br_sem, cs_sem, cr_sem, qp_sem, qs_sem, qr_sem,
):
    x, y, z, k = place()
    row = x * 4 + y
    ready = greet([(d, 0, 0, 0) for d in (2, 1, 3)] + [(0, d, 0, 0) for d in (2, 1, 3)] + [(0, 0, d, 0) for d in (2, 14, 1, 15)] + [(0, 0, 0, 1)])
    own_x = pltpu.make_async_copy(x_ref, xall.at[row], own_sem.at[0])
    own_g = pltpu.make_async_copy(g_ref, gall.at[z, k], own_sem.at[1])
    own_m = pltpu.make_async_copy(m_ref, acc, own_sem.at[2])
    own_x.start()
    own_g.start()
    own_m.start()
    rt[...] = r_ref[...].T
    own_x.wait()
    own_g.wait()
    ready()

    sent = []
    number = 0
    gnum = 0

    def half(which, owner):
        return xall.at[owner, pl.ds(384, 416)] if which else xall.at[owner, pl.ds(0, 384)]

    def pass_on(which, owner, along_x, ds):
        nonlocal number
        sem = xb_sem if which else xa_sem
        for d in ds:
            to = moved(d, 0) if along_x else moved(0, d)
            sent.append(send(half(which, owner), half(which, owner), xs_sem.at[number], sem.at[owner], to))
            number += 1

    def pass_g(owner, ds):
        nonlocal gnum
        for d in ds:
            sent.append(
                send(gall.at[owner, k], gall.at[owner, k], gs_sem.at[gnum], gr_sem.at[owner], moved(0, 0, d))
            )
            gnum += 1

    def cross_g(owner):
        sent.append(send(gall.at[owner, k], gall.at[owner, k], gd_sem.at[owner], gk_sem.at[owner], moved(0, 0, 0, 1)))

    def relay_x(d):
        ox = ((x + 4 - d) % 4) * 4 + y
        oy = x * 4 + (y + 4 - d) % 4
        landed(half(0, ox), xa_sem.at[ox], xs_sem.at[0])
        landed(half(1, oy), xb_sem.at[oy], xs_sem.at[0])
        for e in (1, 3, 2):
            pass_on(0, ox, False, (e,))
            pass_on(1, oy, True, (e,))

    def take_g(owner, ds):
        landed(gall.at[owner, k], gr_sem.at[owner], gs_sem.at[0])
        pass_g(owner, ds)
        cross_g(owner)

    def relay_g(d):
        take_g((z + 16 - d) % 16, (2, 1))
        take_g((z + d) % 16, (14, 15) if d < 6 else (15,))

    pass_g(z, (2, 14, 1, 15))
    for d in (1, 3, 2):
        pass_on(0, row, True, (d,))
        pass_on(1, row, False, (d,))
    cross_g(z)
    for d in (1, 3, 2):
        pass_on(0, row, False, (d,))
        pass_on(1, row, True, (d,))
    relay_g(2)
    relay_x(1)
    relay_g(4)
    relay_x(3)
    relay_x(2)
    relay_g(6)
    for d in (1, 3, 5, 7):
        take_g((z + 16 - d) % 16, ())
        take_g((z + d) % 16, ())
    take_g((z + 8) % 16, ())
    for i in range(16):
        landed(gall.at[i, 1 - k], gk_sem.at[i], gd_sem.at[0])

    own_m.wait()
    for i in range(16):
        gt[i] = gall[i].reshape(128, 320).T
    for d in (0, 1, 3, 2):
        gx, gy = (x + 4 - d) % 4, (y + 4 - d) % 4
        for e in (1, 3, 2):
            owner = gx * 4 + (y + 4 - e) % 4
            landed(half(0, owner), xa_sem.at[owner], xs_sem.at[0])
            owner = ((x + 4 - e) % 4) * 4 + gy
            landed(half(1, owner), xb_sem.at[owner], xs_sem.at[0])
        left = jnp.concatenate([gt[gx * 4 + i] for i in range(4)], axis=1)
        lines = jnp.concatenate([xall[gx * 4 + i, 0:384] for i in range(4)], axis=1)
        acc[:, 0:384] += dot_bf16(left, lines, 1, 1)
        left = jnp.concatenate([gt[i * 4 + gy] for i in range(4)], axis=1)
        lines = jnp.concatenate([xall[i * 4 + gy, 384:800] for i in range(4)], axis=1)
        acc[:, 384:800] += dot_bf16(left, lines, 1, 1)
    moment_copy = pltpu.make_async_copy(acc, moment_ref, own_sem.at[3])
    moment_copy.start()
    other = rt[pl.ds(pl.multiple_of(128 * (1 - k), 128), 128), :]
    sp[1 - k] = dot(other, acc[...], 1, 1).reshape(16, 8, 320)

    c = send(sp.at[1 - k], pair, p_sem.at[0], p_sem.at[1], moved(0, 0, 0, 1))
    own = rt[pl.ds(pl.multiple_of(128 * k, 128), 128), :]
    sp[k] = dot(own, acc[...], 1, 1).reshape(16, 8, 320)
    c.wait()
    cs[...] = sp[k] + pair[...]
    copies = [
        send(cs.at[(z + d) % 16], rs.at[d], zs_sem.at[d], zr_sem.at[d], moved(0, 0, d)) for d in NEAR_Z[::-1]
    ]
    total = cs[z]
    for i in range(15):
        copies[14 - i].wait_recv()
        total = total + rs[NEAR_Z[i]]
    sent += copies
    sall[k, z] = total
    for d in NEAR_Z[::-1]:
        sent.append(send(sall.at[k, z], sall.at[k, z], as_sem.at[d], ar_sem.at[z], moved(0, 0, d)))
    sent.append(send(sall.at[k, z], sall.at[k, z], aks_sem.at[z], akr_sem.at[z], moved(0, 0, 0, 1)))
    for d in NEAR_Z:
        oz = (z + 16 - d) % 16
        landed(sall.at[k, oz], ar_sem.at[oz], as_sem.at[0])
        sent.append(send(sall.at[k, oz], sall.at[k, oz], aks_sem.at[oz], akr_sem.at[oz], moved(0, 0, 0, 1)))
    for i in range(16):
        landed(sall.at[1 - k, i], akr_sem.at[i], aks_sem.at[0])

    s_all = sall[...].reshape(256, 320)
    gp[...] = dot(s_all, s_all, 1, 1).reshape(16, 16, 256)
    copies = []
    for i, (a, b) in enumerate(BALANCED):
        to_row = ((x + a) % 4) * 4 + (y + b) % 4
        copies.append(send(gp.at[to_row], grs.at[i], hs_sem.at[i], hr_sem.at[i], moved(a, b)))
    right_copies = []
    for h in range(2):
        part[h] = dot(sall[h].reshape(128, 320), acc[...], 1, 0).reshape(16, 8, 800)
        right_copies.append([])
        for i, (a, b) in enumerate(BALANCED):
            to_row = ((x + a) % 4) * 4 + (y + b) % 4
            right_copies[h].append(
                send(part.at[h, to_row], brs.at[h, i], bs_sem.at[h, i], br_sem.at[h, i], moved(a, b))
            )
    total = gp[row]
    for i in range(15):
        copies[i].wait_recv()
        total = total + grs[i]
    gall2[row] = total
    sent += copies
    for i, (a, b) in enumerate(BALANCED):
        sent.append(send(gall2.at[row], gall2.at[row], ts_sem.at[i], tr_sem.at[row], moved(a, b)))
    for h in range(2):
        total = part[h, row]
        for i in range(15):
            right_copies[h][i].wait_recv()
            total = total + brs[h, i]
        sent += right_copies[h]
        rall[h, row] = total
        for i, (a, b) in enumerate(BALANCED):
            sent.append(send(rall.at[h, row], rall.at[h, row], cs_sem.at[h, i], cr_sem.at[h, row], moved(a, b)))
    for a, b in XY:
        owner = ((x + 4 - a) % 4) * 4 + (y + 4 - b) % 4
        landed(gall2.at[owner], tr_sem.at[owner], ts_sem.at[0])

    inverse = factor_inverse(gall2[...].reshape(256, 256), ah)
    basis_out[...] = dot(inverse, s_all, 1, 0).T
    for h in range(2):
        for a, b in XY:
            owner = ((x + 4 - a) % 4) * 4 + (y + 4 - b) % 4
            landed(rall.at[h, owner], cr_sem.at[h, owner], cs_sem.at[0, 0])
    right = dot(inverse, rall[...].reshape(256, 800), 1, 0)

    diagonal = lax.broadcasted_iota(jnp.int32, (128, 128), 0) == lax.broadcasted_iota(jnp.int32, (128, 128), 1)
    squares = jnp.sum(right * right, axis=1, keepdims=True)
    for h in range(2):
        line = jnp.where(diagonal, squares[128 * h : 128 * h + 128], 0.0)
        sq[:, 128 * h : 128 * h + 128] = jnp.sum(line, axis=0, keepdims=True)
    c = send(sq, sq2, qp_sem.at[0], qp_sem.at[1], moved(0, 0, 0, 1))
    c.wait()
    sq[...] = sq[...] + sq2[...]
    copies = [send(sq, sqs.at[d], qs_sem.at[d], qr_sem.at[d], moved(0, 0, d)) for d in NEAR_Z[::-1]]
    high_ref[...], low_ref[...] = halves(right)
    right_out[...] = right.T
    total = sq[...]
    for i in range(15):
        copies[14 - i].wait_recv()
        total = total + sqs[NEAR_Z[i]]
    sent += copies
    squares_out[...] = total
    moment_copy.wait()
    for c in sent:
        c.wait_send()


def wide(column):
    return jnp.broadcast_to(column, (8, 128))


def factor_64(tile, parity):
    sub = lax.broadcasted_iota(jnp.int32, (8, 128), 0)
    rows = [tile[8 * t : 8 * t + 8] for t in range(8)]
    for p in range(8):
        first = 64 * parity + 8 * p
        col = {t: [wide(rows[t][:, first + j : first + j + 1]) for j in range(8)] for t in range(p, 8)}
        pivots = jnp.ones((8, 128), f32)
        for j in range(8):
            b = {i: wide(col[p][j][i : i + 1]) for i in range(j, 8)}
            inverse = 1.0 / b[j]
            pivots = jnp.where(sub == j, b[j], pivots)
            line = wide(rows[p][j : j + 1])
            for t in range(p, 8):
                factor = col[t][j] * inverse
                for i in range(j + 1, 8):
                    col[t][i] = col[t][i] - factor * b[i]
                if t == p:
                    factor = jnp.where(sub > j, factor, 0.0)
                rows[t] = rows[t] - factor * line
        rows[p] = rows[p] * lax.rsqrt(pivots)
    return jnp.concatenate(rows, axis=0)


def factor_inverse(gram, ah):
    ah[:, 0:256] = gram
    lines = lax.broadcasted_iota(jnp.int32, (256, 256), 0)
    ah[:, 256:512] = jnp.where(lines == lax.broadcasted_iota(jnp.int32, (256, 256), 1), 1.0, 0.0)
    done = []
    lane = lax.broadcasted_iota(jnp.int32, (64, 128), 1)
    line = lax.broadcasted_iota(jnp.int32, (64, 128), 0)
    for b in range(4):
        parity, low = b % 2, 64 * b
        own = (lane // 64) == parity
        unit = jnp.where(lane == line + 64 * (1 - parity), 1.0, 0.0)
        tile = jnp.where(own, ah[low : low + 64, 128 * (b // 2) : 128 * (b // 2) + 128], unit)
        inverse = jnp.where(own, 0.0, factor_64(tile, parity))
        first = 128 * ((b + 1) // 2)
        block = ah[low : low + 64, first:512]
        upper = dot(inverse, jnp.concatenate([block, block], axis=0), 1, 0)
        done.append(upper[:, 256 - first :])
        if b < 3:
            change = dot(upper[:, : 256 - first], upper, 0, 0)
            ah[low + 64 : 256, first:512] = ah[low + 64 : 256, first:512] - change[low + 64 - first :, :]
    return jnp.concatenate(done, axis=0)


def update_kernel(w_ref, moment_ref, basis_ref, high_ref, low_ref, right_ref, squares_ref, w_out, m_out, f_out):
    scale = lax.rsqrt(squares_ref[...] / N + tiny_eps)
    f_out[...] = right_ref[...] * scale

    def product(left):
        high, low = halves(left)
        rest = dot_bf16(high, low_ref[...], 1, 0) + dot_bf16(low, high_ref[...], 1, 0)
        return dot_bf16(high, high_ref[...], 1, 0) + rest

    basis = basis_ref[...]
    m_out[...] = moment_ref[...] - (1.0 - mix_rate) * product(basis)
    w_out[...] = w_ref[...].astype(f32) * (1.0 - step_rate * weight_decay) - step_rate * math.sqrt(
        M / RANK
    ) * product(basis * scale)


def vmem(count):
    return [pl.BlockSpec(memory_space=pltpu.VMEM)] * count


def shape(*dims):
    return jax.ShapeDtypeStruct(dims, f32)


def on_device(inputs, out_grads, weights, momentum, right_factor):
    dma = pltpu.SemaphoreType.DMA
    moment, basis, high, low, right, squares = pl.pallas_call(
        step_kernel,
        name="step",
        out_shape=(
            shape(320, 800),
            shape(320, 256),
            jax.ShapeDtypeStruct((256, 800), bf16),
            jax.ShapeDtypeStruct((256, 800), bf16),
            shape(800, 256),
            shape(1, 256),
        ),
        in_specs=vmem(2) + [pl.BlockSpec(memory_space=pl.ANY)] + vmem(1),
        out_specs=(pl.BlockSpec(memory_space=pl.ANY), *vmem(5)),
        scratch_shapes=[
            pltpu.VMEM((16, 800, 128), bf16),
            pltpu.VMEM((16, 2, 64, 320), bf16),
            pltpu.VMEM((16, 320, 128), bf16),
            pltpu.VMEM((256, 800), f32),
            pltpu.VMEM((320, 800), f32),
            pltpu.VMEM((2, 16, 8, 320), f32),
            pltpu.VMEM((16, 8, 320), f32),
            pltpu.VMEM((16, 8, 320), f32),
            pltpu.VMEM((16, 8, 320), f32),
            pltpu.VMEM((2, 16, 8, 320), f32),
            pltpu.VMEM((16, 16, 256), f32),
            pltpu.VMEM((15, 16, 256), f32),
            pltpu.VMEM((16, 16, 256), f32),
            pltpu.VMEM((256, 512), f32),
            pltpu.VMEM((2, 16, 8, 800), f32),
            pltpu.VMEM((2, 15, 8, 800), f32),
            pltpu.VMEM((2, 16, 8, 800), f32),
            pltpu.VMEM((1, 256), f32),
            pltpu.VMEM((1, 256), f32),
            pltpu.VMEM((16, 1, 256), f32),
            dma((4,)), dma((30,)), dma((16,)), dma((16,)), dma((18,)), dma((16,)), dma((16,)), dma((16,)),
            dma((2,)), dma((16,)), dma((16,)), dma((16,)), dma((16,)), dma((16,)), dma((16,)),
            dma((15,)), dma((15,)), dma((15,)), dma((16,)),
            dma((2, 15)), dma((2, 15)), dma((2, 15)), dma((2, 16)),
            dma((2,)), dma((16,)), dma((16,)),
        ],
        compiler_params=pltpu.CompilerParams(collective_id=0, has_side_effects=True, vmem_limit_bytes=VMEM_LIMIT),
    )(inputs.T, out_grads, momentum, right_factor)
    lines, whole = (lambda i: (i, 0)), (lambda i: (0, 0))
    return tuple(
        pl.pallas_call(
            update_kernel,
            name="updates",
            grid=(4,),
            out_shape=(shape(320, 800), shape(320, 800), shape(800, 256)),
            in_specs=[
                pl.BlockSpec((80, 800), lines),
                pl.BlockSpec((80, 800), lines),
                pl.BlockSpec((80, 256), lines),
                pl.BlockSpec((256, 800), whole),
                pl.BlockSpec((256, 800), whole),
                pl.BlockSpec((200, 256), lines),
                pl.BlockSpec((1, 256), whole),
            ],
            out_specs=(
                pl.BlockSpec((80, 800), lines),
                pl.BlockSpec((80, 800), lines),
                pl.BlockSpec((200, 256), lines),
            ),
            compiler_params=pltpu.CompilerParams(vmem_limit_bytes=VMEM_LIMIT),
        )(weights, moment, basis, high, low, right, squares)
    )


def solution(mesh):
    return jax.shard_map(
        on_device,
        mesh=mesh,
        in_specs=(P("row", "col"), P("col", "row"), P("row", "col"), P("row", "col"), P("col", None)),
        out_specs=(P("row", "col"), P("row", "col"), P("col", None)),
        check_vma=False,
    )
```
